128 devices in a mesh: wide: 16 (over x_hi, z, core), narrow: 8 (over y, x_lo).
Axes of the slice: x: 4 (x_hi: 2, x_lo: 2; x = x_hi * 2 + x_lo), y: 4, z: 4, core: 2. Of those that a mesh axis runs over, the one named last changes fastest.
Arguments:
- prompt_states: bfloat16 [384, 4096], P('wide'), may hold values from -6 to 6
- prompt_lengths: int32 [1], replicated, may hold values from 96 to 384
- feed_gain: float32 [4096], replicated, may hold values from 0.1 to 1.9
- gate_weight: bfloat16 [4096, 5120], P(None, 'narrow'), may hold values from -0.09375 to 0.09375
- up_weight: bfloat16 [4096, 5120], P(None, 'narrow'), may hold values from -0.09375 to 0.09375
- down_weight: bfloat16 [5120, 4096], P('narrow'), may hold values from -0.078125 to 0.078125
- final_gain: float32 [4096], replicated, may hold values from 0.1 to 1.9
- key_weight: bfloat16 [4096, 3072], P(None, 'narrow'), may hold values from -0.09375 to 0.09375
- value_weight: bfloat16 [4096, 3072], P(None, 'narrow'), may hold values from -0.09375 to 0.09375
- prompt_key_gain: float32 [3072], P('narrow'), may hold values from 1 to 2.6
- latent_queries: bfloat16 [16384, 3072], P(('wide', 'narrow')), may hold values from -6 to 6
- latent_keys: bfloat16 [16384, 3072], P(('wide', 'narrow')), may hold values from -6 to 6
- latent_values: bfloat16 [16384, 3072], P(('wide', 'narrow')), may hold values from -4 to 4
- cross_queries: bfloat16 [16384, 3072], P(('wide', 'narrow')), may hold values from -6 to 6
- query_gain: float32 [3072], replicated, may hold values from 1 to 2.6
- key_gain: float32 [3072], replicated, may hold values from 1 to 2.6
- cross_query_gain: float32 [3072], replicated, may hold values from 1 to 2.6
Outputs:
- self_out: bfloat16 [16384, 3072], P('wide', 'narrow')
- cross_out: bfloat16 [16384, 3072], P('wide', 'narrow')
The draws below stay inside these ranges and needn't reach their ends.
Inputs may be any that keep to these rules, and one draw needn't show every extreme that they name: `prompt_lengths`: the number of live prompt tokens; later prompt positions are padding.
All inputs are finite; a program needn't handle non-finite values.
Results may differ from the reference program's by a relative error of at most 0.017.
Values may be sent and summed in bfloat16 or wider, within the bound.
No kernel may reach another device: no remote copies, remote signals or barrier semaphores. Data moves between devices by JAX's collectives and lax.ppermute only.
A program may use at most 192 MiB of HBM per device.

```python
import math
import jax
import jax.numpy as jnp
from jax import lax

DT = 4096
FFT = 5120
HEADS = 24
HEAD_DIM = 128
HD = 3072
SEQ = 16384
PROMPT = 384


def block_levels(stream_key, dims, shards, least, high):
    loudness, own = 1.0, jax.random.fold_in(stream_key, 6)
    for axis_at, parts in shards:
        steps = jnp.exp(jax.random.uniform(jax.random.fold_in(own, axis_at), (parts,), jnp.float32, least / len(shards), high / len(shards)))
        loudness = loudness * jnp.repeat(steps, dims[axis_at] // parts).reshape([-1 if axis == axis_at else 1 for axis in range(len(dims))])
    return loudness


def normal_values(rng, extent, scale, limit, cuts=(), kind=jnp.bfloat16):
    level = block_levels(rng, extent, cuts, -0.22, 0.18) if cuts else 1.0
    drawn = jax.random.normal(rng, extent, jnp.float32) * scale * level
    return jnp.minimum(jnp.maximum(drawn, -limit), limit).astype(kind)


def setup_inputs(seed: int = 0) -> dict:
    splits = jax.random.split(jax.random.key(seed), 18)
    return {
        "prompt_states": normal_values(splits[0], (PROMPT, DT), 1.0, 6.0, ((0, 16),)),
        "prompt_lengths": jax.random.randint(splits[1], (1,), PROMPT // 4, PROMPT + 1).astype(jnp.int32),
        "feed_gain": jnp.clip(1.0 + 0.18 * jax.random.normal(splits[2], (DT,), jnp.float32), 0.1, 1.9),
        "gate_weight": normal_values(splits[3], (DT, FFT), DT ** -0.5, 0.09375, ((1, 8),)),
        "up_weight": normal_values(splits[4], (DT, FFT), DT ** -0.5, 0.09375, ((1, 8),)),
        "down_weight": normal_values(splits[5], (FFT, DT), FFT ** -0.5, 0.078125, ((0, 8),)),
        "final_gain": jnp.clip(1.0 + 0.18 * jax.random.normal(splits[6], (DT,), jnp.float32), 0.1, 1.9),
        "key_weight": normal_values(splits[7], (DT, HD), DT ** -0.5, 0.09375, ((1, 8),)),
        "value_weight": normal_values(splits[8], (DT, HD), DT ** -0.5, 0.09375, ((1, 8),)),
        "prompt_key_gain": jnp.clip(jnp.exp(math.log(2.6) - 0.9555114 * jax.random.uniform(splits[9], (HD,), jnp.float32) ** block_levels(splits[9], (HD,), ((0, 8),), -0.2, 0.2)), 1.0, 2.6),
        "latent_queries": normal_values(splits[10], (SEQ, HD), 1.0, 6.0, ((0, 128),)),
        "latent_keys": normal_values(splits[11], (SEQ, HD), 1.0, 6.0, ((0, 128),)),
        "latent_values": normal_values(splits[12], (SEQ, HD), 1.0, 4.0, ((0, 128),)),
        "cross_queries": normal_values(splits[13], (SEQ, HD), 1.0, 6.0, ((0, 128),)),
        "query_gain": jnp.clip(jnp.exp(jax.random.uniform(splits[14], (HD,), jnp.float32, math.log(1.0), math.log(2.6))), 1.0, 2.6),
        "key_gain": jnp.clip(jnp.exp(jax.random.uniform(splits[15], (HD,), jnp.float32, math.log(1.0), math.log(2.6))), 1.0, 2.6),
        "cross_query_gain": jnp.clip(jnp.exp(jax.random.uniform(splits[16], (HD,), jnp.float32, math.log(1.0), math.log(2.6))), 1.0, 2.6),
    }


epsilon = 1e-06
tile_rows = 1024

def rms_rows(values, gain):
    widened = values.astype(jnp.float32)
    inverse = lax.rsqrt(lax.optimization_barrier(jnp.mean(widened * widened, axis=-1, keepdims=True)) + epsilon)
    return widened * inverse * gain

def head_norm(values, gain, head_size):
    count, width = values.shape
    split = values.astype(jnp.float32).reshape(count, width // head_size, head_size)
    inverse = lax.rsqrt(lax.optimization_barrier(jnp.mean(split * split, axis=-1, keepdims=True)) + epsilon)
    return (split * inverse).reshape(count, width) * gain

def attend_rows(queries, keys, values, live):
    factor = 1.0 / math.sqrt(queries.shape[-1])
    scores = jnp.dot(queries, keys.T, preferred_element_type=jnp.float32) * factor
    weights = jnp.where(live[None, :], jnp.exp(scores), 0.0)
    totals = lax.optimization_barrier(jnp.sum(weights, axis=-1, keepdims=True))
    summed = jnp.dot(weights.astype(jnp.bfloat16), values, preferred_element_type=jnp.float32)
    return summed / totals

def attention(queries, keys, values, live):
    length = queries.shape[0]

    def split_heads(array):
        return array.reshape(array.shape[0], HEADS, HEAD_DIM).transpose(1, 0, 2)
    block_rows = math.gcd(length, tile_rows)

    def one_head(operands):
        query_head, key_head, value_head = operands
        blocks = query_head.reshape(length // block_rows, block_rows, HEAD_DIM)
        result = lax.map(lambda block: attend_rows(block, key_head, value_head, live), blocks)
        return result.reshape(length, HEAD_DIM)
    result = lax.map(one_head, (split_heads(queries), split_heads(keys), split_heads(values)))
    return result.transpose(1, 0, 2).reshape(length, HEADS * HEAD_DIM).astype(jnp.bfloat16)

def reference(prompt_states, prompt_lengths, feed_gain, gate_weight, up_weight, down_weight, final_gain, key_weight, value_weight, prompt_key_gain, latent_queries, latent_keys, latent_values, cross_queries, query_gain, key_gain, cross_query_gain):
    normed = rms_rows(prompt_states, feed_gain).astype(jnp.bfloat16)
    gate = jnp.dot(normed, gate_weight, preferred_element_type=jnp.float32)
    upward = jnp.dot(normed, up_weight, preferred_element_type=jnp.float32)
    hidden = (jax.nn.gelu(gate, approximate=True) * upward).astype(jnp.bfloat16)
    feed_out = jnp.dot(hidden, down_weight, preferred_element_type=jnp.float32)
    text = rms_rows(prompt_states.astype(jnp.float32) + feed_out, final_gain).astype(jnp.bfloat16)
    prompt_keys = head_norm(jnp.dot(text, key_weight, preferred_element_type=jnp.float32), prompt_key_gain, HEAD_DIM).astype(jnp.bfloat16)
    prompt_values = jnp.dot(text, value_weight, preferred_element_type=jnp.float32).astype(jnp.bfloat16)
    queries = head_norm(latent_queries, query_gain, HEAD_DIM).astype(jnp.bfloat16)
    keys = head_norm(latent_keys, key_gain, HEAD_DIM).astype(jnp.bfloat16)
    cross = head_norm(cross_queries, cross_query_gain, HEAD_DIM).astype(jnp.bfloat16)
    all_live = jnp.ones((latent_keys.shape[0],), dtype=bool)
    self_out = attention(queries, keys, latent_values, all_live)
    prompt_live = jnp.arange(prompt_keys.shape[0], dtype=jnp.int32) < prompt_lengths[0]
    cross_out = attention(cross, prompt_keys, prompt_values, prompt_live)
    return (self_out, cross_out)
```

```python
import math

import jax
import jax.numpy as jnp
from jax import lax
from jax.experimental import pallas as pl
from jax.experimental.pallas import tpu as pltpu
from jax.sharding import PartitionSpec as P

HEAD = 128
EPS = 1e-06
SCALE = math.log2(math.e) / math.sqrt(HEAD)
TILE = 512
CHUNK = 2048
EXTRA = 16


def vmem(mib):
    return pltpu.CompilerParams(vmem_limit_bytes=mib * 2**20)


def pack_kernel(q_ref, k_ref, v_ref, c_ref, qg_ref, kg_ref, cg_ref, *outs):
    heads = len(outs) // 2

    def norm(ref, gain_ref, h, factor):
        x = ref[:, h * HEAD : (h + 1) * HEAD].astype(jnp.float32)
        inverse = lax.rsqrt(jnp.mean(x * x, axis=-1, keepdims=True) + EPS)
        gain = gain_ref[:, h * HEAD : (h + 1) * HEAD] * factor
        return (x * inverse * gain).astype(jnp.bfloat16)

    c_out = outs[-1]
    for h in range(heads):
        kv_out, q_out = outs[2 * h], outs[2 * h + 1]
        kv_out[0, :HEAD, :] = norm(k_ref, kg_ref, h, 1.0)
        v = v_ref[:, h * HEAD : (h + 1) * HEAD].astype(jnp.float32)
        kv_out[0, HEAD:, :] = v.T.astype(jnp.bfloat16)
        q_out[0] = norm(q_ref, qg_ref, h, SCALE)
        c_out[0, h * HEAD : (h + 1) * HEAD, :] = norm(c_ref, cg_ref, h, SCALE)


def pack(q, k, v, c, qg, kg, cg, groups):
    rows, width = q.shape
    part = width // groups
    heads = part // HEAD
    block = pl.BlockSpec((rows, part), lambda n: (0, n))
    gain = pl.BlockSpec((1, part), lambda n: (0, n))
    shapes, specs = [], []
    for depth in (2 * HEAD, rows) * heads + (heads * rows,):
        shapes.append(jax.ShapeDtypeStruct((groups, depth, HEAD), jnp.bfloat16))
        specs.append(pl.BlockSpec((1, depth, HEAD), lambda n: (n, 0, 0)))
    return pl.pallas_call(
        pack_kernel,
        grid=(groups,),
        in_specs=[block] * 4 + [gain] * 3,
        out_specs=specs,
        out_shape=shapes,
        compiler_params=vmem(32),
        cost_estimate=pl.CostEstimate(
            flops=8 * q.size * 4, bytes_accessed=16 * q.size, transcendentals=0
        ),
        name="pack",
    )(q, k, v, c, qg[None, :], kg[None, :], cg[None, :])


def attend_kernel(nq, nkv, *refs):
    q_in, kv_in = refs[:nq], refs[nq : nq + nkv]
    outs = refs[nq + nkv : 2 * nq + nkv]
    q_s, k_s, v_s, o_s, sems = refs[2 * nq + nkv :]
    blocks = q_in[0].shape[0]
    copies = []
    for i, ref in enumerate(q_in):
        copies.append((ref, q_s.at[pl.ds(i * blocks, blocks)]))
    for i, ref in enumerate(kv_in):
        copies.append((ref.at[:, pl.ds(0, HEAD), :], k_s.at[pl.ds(i * blocks, blocks)]))
        copies.append((ref.at[:, pl.ds(HEAD, HEAD), :], v_s.at[pl.ds(i * blocks, blocks)]))
    copies = [
        pltpu.make_async_copy(src, dst, sems.at[i]) for i, (src, dst) in enumerate(copies)
    ]
    for copy in copies:
        copy.start()
    for copy in copies:
        copy.wait()
    per_q = TILE // HEAD
    per_k = CHUNK // HEAD
    per_block = blocks // per_q

    def tile(t, _):
        q = q_s[pl.ds(t * per_q, per_q)].reshape(TILE, HEAD)
        acc = jnp.zeros((HEAD, TILE), jnp.float32)
        total = jnp.zeros((8, TILE), jnp.float32)
        for j in range(nkv * blocks // per_k):
            keys = k_s[j * per_k : (j + 1) * per_k].reshape(CHUNK, HEAD)
            s = lax.dot_general(
                keys, q, (((1,), (1,)), ((), ())), preferred_element_type=jnp.float32
            )
            p = jnp.exp2(s)
            total = total + jnp.sum(p.reshape(CHUNK // 8, 8, TILE), axis=0)
            values = jnp.concatenate(
                [v_s[j * per_k + i] for i in range(per_k)], axis=1
            )
            acc = acc + jnp.dot(
                values, p.astype(jnp.bfloat16), preferred_element_type=jnp.float32
            )
        row = jnp.sum(total, axis=0, keepdims=True)
        high = row.astype(jnp.bfloat16).astype(jnp.float32)
        words = jnp.concatenate(
            [jnp.broadcast_to(high, (8, TILE)), jnp.broadcast_to(row - high, (8, TILE))], axis=0
        )
        columns = pl.ds(pl.multiple_of((t % per_block) * TILE, TILE), TILE)
        o_s[t // per_block, :HEAD, columns] = acc.astype(jnp.bfloat16)
        o_s[t // per_block, HEAD:, columns] = words.astype(jnp.bfloat16)
        return 0

    lax.fori_loop(0, nq * per_block, tile, 0)
    copies = [
        pltpu.make_async_copy(o_s.at[i], ref, sems.at[i]) for i, ref in enumerate(outs)
    ]
    for copy in copies:
        copy.start()
    for copy in copies:
        copy.wait()


def attend(queries, pairs):
    nq, nkv = len(queries), len(pairs)
    blocks = queries[0].shape[0]
    count = blocks * HEAD
    shape = jax.ShapeDtypeStruct((HEAD + EXTRA, count), jnp.bfloat16)
    work = nq * nkv * count * count
    return pl.pallas_call(
        lambda *refs: attend_kernel(nq, nkv, *refs),
        in_specs=[pl.BlockSpec(memory_space=pl.ANY)] * (nq + nkv),
        out_specs=[pl.BlockSpec(memory_space=pl.ANY)] * nq,
        out_shape=[shape] * nq,
        scratch_shapes=[
            pltpu.VMEM((nq * blocks, HEAD, HEAD), jnp.bfloat16),
            pltpu.VMEM((nkv * blocks, HEAD, HEAD), jnp.bfloat16),
            pltpu.VMEM((nkv * blocks, HEAD, HEAD), jnp.bfloat16),
            pltpu.VMEM((nq, HEAD + EXTRA, count), jnp.bfloat16),
            pltpu.SemaphoreType.DMA((nq + 2 * nkv,)),
        ],
        compiler_params=vmem(48),
        cost_estimate=pl.CostEstimate(
            flops=4 * HEAD * work, bytes_accessed=6 * 2**20, transcendentals=work
        ),
        name="attend",
    )(*queries, *pairs)


def merge_kernel(parts, *refs):
    out_ref = refs[-1]
    for h in range((len(refs) - 1) // parts):
        group = refs[h * parts : (h + 1) * parts]
        weighted = sum(ref[:HEAD, :].astype(jnp.float32) for ref in group)
        words = sum(ref[HEAD:, :].astype(jnp.float32) for ref in group)
        total = words[0:1] + words[8:9]
        out_ref[:, h * HEAD : (h + 1) * HEAD] = (weighted / total).T.astype(jnp.bfloat16)


def merge(groups):
    parts, heads = len(groups[0]), len(groups)
    rows, count = groups[0][0].shape
    step = 256
    return pl.pallas_call(
        lambda *refs: merge_kernel(parts, *refs),
        grid=(count // step,),
        in_specs=[pl.BlockSpec((rows, step), lambda i: (0, i))] * (parts * heads),
        out_specs=pl.BlockSpec((step, heads * HEAD), lambda i: (i, 0)),
        out_shape=jax.ShapeDtypeStruct((count, heads * HEAD), jnp.bfloat16),
        compiler_params=vmem(32),
        cost_estimate=pl.CostEstimate(
            flops=count * heads * HEAD * 8, bytes_accessed=4 * 2**20, transcendentals=0
        ),
        name="merge",
    )(*[a for group in groups for a in group])


def cross_kernel(length_ref, c_ref, kv_ref, out_ref):
    live = length_ref[0]
    blocks = c_ref.shape[0]
    heads = c_ref.shape[1] // HEAD
    count = kv_ref.shape[0]
    for h in range(heads):
        keys = kv_ref[:, h * HEAD : (h + 1) * HEAD]
        values = kv_ref[:, (heads + h) * HEAD : (heads + h + 1) * HEAD]
        values = values.astype(jnp.float32).T.astype(jnp.bfloat16)
        q = c_ref[:, h * HEAD : (h + 1) * HEAD, :].reshape(blocks * HEAD, HEAD)
        s = lax.dot_general(
            keys, q, (((1,), (1,)), ((), ())), preferred_element_type=jnp.float32
        )
        row = lax.broadcasted_iota(jnp.int32, s.shape, 0)
        p = jnp.where(row < live, jnp.exp2(s), 0.0)
        total = jnp.sum(p, axis=0, keepdims=True)
        weighted = jnp.dot(values, p.astype(jnp.bfloat16), preferred_element_type=jnp.float32)
        out_ref[:, h * HEAD : (h + 1) * HEAD] = (weighted / total).T.astype(jnp.bfloat16)


def cross(lengths, c, kv):
    blocks, depth, _ = c.shape
    step = 4
    heads = depth // HEAD
    return pl.pallas_call(
        cross_kernel,
        grid=(blocks // step,),
        in_specs=[
            pl.BlockSpec(memory_space=pltpu.SMEM),
            pl.BlockSpec((step, depth, HEAD), lambda i: (i, 0, 0)),
            pl.BlockSpec(kv.shape, lambda i: (0, 0)),
        ],
        out_specs=pl.BlockSpec((step * HEAD, depth), lambda i: (i, 0)),
        out_shape=jax.ShapeDtypeStruct((blocks * HEAD, depth), jnp.bfloat16),
        compiler_params=vmem(32),
        cost_estimate=pl.CostEstimate(
            flops=4 * HEAD * heads * blocks * HEAD * kv.shape[0],
            bytes_accessed=3 * 2**20,
            transcendentals=heads * blocks * HEAD * kv.shape[0],
        ),
        name="cross",
    )(lengths, c, kv)


def rms_rows(values, gain):
    widened = values.astype(jnp.float32)
    inverse = lax.rsqrt(jnp.mean(widened * widened, axis=-1, keepdims=True) + EPS)
    return widened * inverse * gain


def head_norm(values, gain):
    count, width = values.shape
    split = values.reshape(count, width // HEAD, HEAD)
    inverse = lax.rsqrt(jnp.mean(split * split, axis=-1, keepdims=True) + EPS)
    return (split * inverse).reshape(count, width) * gain


def wide_pairs(move):
    pairs = []
    for hi in range(2):
        for z in range(4):
            for core in range(2):
                to_hi, to_z, to_core = move(hi, z, core)
                pairs.append((hi * 8 + z * 2 + core, to_hi * 8 + (to_z % 4) * 2 + to_core))
    return pairs


UP = wide_pairs(lambda hi, z, core: (hi, z + 1, core))
DOWN = wide_pairs(lambda hi, z, core: (hi, z + 3, core))
ACROSS = wide_pairs(lambda hi, z, core: (hi, z + 2, core))
OTHER_X = wide_pairs(lambda hi, z, core: (1 - hi, z, core))
OTHER_CORE = wide_pairs(lambda hi, z, core: (hi, z, 1 - core))


def send(array, pairs):
    return lax.ppermute(array, "wide", pairs)


def trade(array):
    return lax.all_to_all(array, "narrow", split_axis=0, concat_axis=0, tiled=True)


def body(
    prompt_states,
    prompt_lengths,
    feed_gain,
    gate_weight,
    up_weight,
    down_weight,
    final_gain,
    key_weight,
    value_weight,
    prompt_key_gain,
    latent_queries,
    latent_keys,
    latent_values,
    cross_queries,
    query_gain,
    key_gain,
    cross_query_gain,
):
    groups = latent_queries.shape[1] // key_weight.shape[1]
    packed = pack(
        latent_queries,
        latent_keys,
        latent_values,
        cross_queries,
        query_gain,
        key_gain,
        cross_query_gain,
        groups,
    )
    heads = len(packed) // 2

    normed = rms_rows(prompt_states, feed_gain).astype(jnp.bfloat16)
    gate = jnp.dot(normed, gate_weight, preferred_element_type=jnp.float32)
    upward = jnp.dot(normed, up_weight, preferred_element_type=jnp.float32)
    hidden = (jax.nn.gelu(gate, approximate=True) * upward).astype(jnp.bfloat16)
    partial_out = jnp.dot(hidden, down_weight, preferred_element_type=jnp.float32)
    rows, width = partial_out.shape
    part = width // groups
    pieces = partial_out.reshape(rows, groups, part).transpose(1, 0, 2)
    feed_piece = jnp.sum(trade(pieces), axis=0)
    mine = lax.axis_index("narrow") * part
    summed_piece = (
        lax.dynamic_slice_in_dim(prompt_states, mine, part, axis=1).astype(jnp.float32)
        + feed_piece
    )
    summed = trade(jnp.broadcast_to(summed_piece[None], (groups, rows, part)))
    summed = summed.transpose(1, 0, 2).reshape(rows, width)
    text = rms_rows(summed, final_gain).astype(jnp.bfloat16)
    prompt_keys = head_norm(
        jnp.dot(text, key_weight, preferred_element_type=jnp.float32), prompt_key_gain
    ).astype(jnp.bfloat16)
    prompt_values = jnp.dot(text, value_weight, preferred_element_type=jnp.float32).astype(
        jnp.bfloat16
    )
    prompt_pair = lax.all_gather(
        jnp.concatenate([prompt_keys, prompt_values], axis=1), "wide", axis=0, tiled=True
    )

    results = []
    for h in range(heads):
        pair, query = trade(packed[2 * h]), trade(packed[2 * h + 1])
        pair_x = send(pair, OTHER_X)
        pairs = [pair, send(pair, OTHER_CORE), pair_x, send(pair_x, OTHER_CORE)]
        queries = [query, send(query, UP), send(query, DOWN), send(query, ACROSS)]
        own, below, above, across = attend(queries, pairs)
        results.append([own, send(below, DOWN), send(above, UP), send(across, ACROSS)])
    crossed = trade(packed[-1])
    cross_out = cross(prompt_lengths, crossed, prompt_pair)
    self_out = merge(results)
    return (self_out, cross_out)


def solution(mesh):
    rows = P(("wide", "narrow"), None)
    return jax.shard_map(
        body,
        mesh=mesh,
        in_specs=(
            P("wide", None),
            P(),
            P(),
            P(None, "narrow"),
            P(None, "narrow"),
            P("narrow", None),
            P(),
            P(None, "narrow"),
            P(None, "narrow"),
            P("narrow"),
            rows,
            rows,
            rows,
            rows,
            P(),
            P(),
            P(),
        ),
        out_specs=(P("wide", "narrow"), P("wide", "narrow")),
        check_vma=False,
    )
```

```python
import math

import jax
import jax.numpy as jnp
from jax import lax
from jax.experimental import pallas as pl
from jax.experimental.pallas import tpu as pltpu
from jax.sharding import PartitionSpec as P

HEAD = 128
EPS = 1e-06
SCALE = math.log2(math.e) / math.sqrt(HEAD)
TILE = 512
CHUNK = 2048
EXTRA = 16
SLOT = 32


def vmem(mib):
    return pltpu.CompilerParams(vmem_limit_bytes=mib * 2**20)


def normed(ref, gain_ref, at, factor):
    x = ref[:, at].astype(jnp.float32)
    inverse = lax.rsqrt(jnp.mean(x * x, axis=-1, keepdims=True) + EPS)
    return (x * inverse * (gain_ref[:, at] * factor)).astype(jnp.bfloat16)


def pack_kernel(heads, plan, q_ref, k_ref, v_ref, qg_ref, kg_ref, *rest):
    groups = rest[-1].shape[0]
    outs = rest[2:] if plan["crossed"] else rest

    def group(n, _):
        for h, out, base in plan["heads"]:
            at = pl.ds(pl.multiple_of((n * heads + h) * HEAD, HEAD), HEAD)
            ref = outs[out]
            ref[n, base : base + HEAD, :] = normed(k_ref, kg_ref, at, 1.0)
            ref[n, base + HEAD : base + 2 * HEAD, :] = (
                v_ref[:, at].astype(jnp.float32).T.astype(jnp.bfloat16)
            )
            ref[n, base + 2 * HEAD : base + 3 * HEAD, :] = normed(q_ref, qg_ref, at, SCALE)
        for h, out, base in plan["crossed"]:
            at = pl.ds(pl.multiple_of((n * heads + h) * HEAD, HEAD), HEAD)
            outs[out][n, base : base + HEAD, :] = normed(rest[0], rest[1], at, SCALE)
        return 0

    lax.fori_loop(0, groups, group, 0)


def pack(arrays, gains, groups, heads, plan, depths):
    whole = pl.BlockSpec(memory_space=pltpu.VMEM)
    operands = list(arrays[:3]) + [gain[None, :] for gain in gains[:2]]
    if plan["crossed"]:
        operands += [arrays[3], gains[2][None, :]]
    units = 3 * len(plan["heads"]) + len(plan["crossed"])
    return pl.pallas_call(
        lambda *refs: pack_kernel(heads, plan, *refs),
        in_specs=[whole] * len(operands),
        out_specs=[whole] * len(depths),
        out_shape=[
            jax.ShapeDtypeStruct((groups, depth, HEAD), jnp.bfloat16) for depth in depths
        ],
        compiler_params=vmem(56),
        cost_estimate=pl.CostEstimate(
            flops=8 * arrays[0].size, bytes_accessed=units * 2**20, transcendentals=0
        ),
        name="pack",
    )(*operands)


def words(block):
    high = block.astype(jnp.bfloat16)
    return high, (block - high.astype(jnp.float32)).astype(jnp.bfloat16)


def feed_kernel(x_ref, gain_ref, gate_ref, up_ref, down_ref, out_ref, rows_ref, total):
    step = pl.program_id(0)

    @pl.when(step == 0)
    def _():
        x = x_ref[...].astype(jnp.float32)
        inverse = lax.rsqrt(jnp.mean(x * x, axis=-1, keepdims=True) + EPS)
        rows = x * inverse * gain_ref[...]
        spare = jnp.zeros((SLOT - x.shape[0], x.shape[1]), jnp.float32)
        rows_ref[...] = jnp.concatenate([rows, spare], axis=0).astype(jnp.bfloat16)
        total[...] = jnp.zeros_like(total)

    rows = rows_ref[...]
    gate = jnp.dot(rows, gate_ref[...], preferred_element_type=jnp.float32)
    upward = jnp.dot(rows, up_ref[...], preferred_element_type=jnp.float32)
    hidden = (jax.nn.gelu(gate, approximate=True) * upward).astype(jnp.bfloat16)
    total[...] += jnp.dot(hidden, down_ref[...], preferred_element_type=jnp.float32)

    @pl.when(step == pl.num_programs(0) - 1)
    def _():
        groups = out_ref.shape[0]
        each = total.shape[1] // groups // HEAD
        for n in range(groups):
            for j in range(each):
                at = (n * each + j) * HEAD
                high, low = words(total[:, at : at + HEAD])
                out_ref[n, j * SLOT : (j + 1) * SLOT, :] = high
                out_ref[n, (each + j) * SLOT : (each + j + 1) * SLOT, :] = low


def feed(x, gain, gate, up, down, groups, extra):
    width, hidden = gate.shape
    tile = HEAD
    return pl.pallas_call(
        feed_kernel,
        grid=(hidden // tile,),
        in_specs=[
            pl.BlockSpec(x.shape, lambda i: (0, 0)),
            pl.BlockSpec((1, width), lambda i: (0, 0)),
            pl.BlockSpec((width, tile), lambda i: (0, i)),
            pl.BlockSpec((width, tile), lambda i: (0, i)),
            pl.BlockSpec((tile, width), lambda i: (i, 0)),
        ],
        out_specs=pl.BlockSpec((groups, extra, HEAD), lambda i: (0, 0, 0)),
        out_shape=jax.ShapeDtypeStruct((groups, extra, HEAD), jnp.bfloat16),
        scratch_shapes=[
            pltpu.VMEM((SLOT, width), jnp.bfloat16),
            pltpu.VMEM((SLOT, width), jnp.float32),
        ],
        compiler_params=vmem(56),
        cost_estimate=pl.CostEstimate(
            flops=6 * SLOT * width * hidden,
            bytes_accessed=6 * width * hidden,
            transcendentals=SLOT * hidden,
        ),
        name="feed",
    )(x, gain[None, :], gate, up, down)


def fold_kernel(parts_ref, _, out_ref):
    groups, depth, _ = parts_ref.shape
    half = depth // 2
    total = jnp.zeros((half, HEAD), jnp.float32)
    for n in range(groups):
        total = total + parts_ref[n, :half, :].astype(jnp.float32)
        total = total + parts_ref[n, half:, :].astype(jnp.float32)
    high, low = words(total)
    for n in range(groups):
        out_ref[n, :half, :] = high
        out_ref[n, half:, :] = low


def fold(parts, into):
    block = pl.BlockSpec(parts.shape, lambda i: (0, 0, 0))
    return pl.pallas_call(
        fold_kernel,
        grid=(1,),
        in_specs=[block, pl.BlockSpec(memory_space=pl.ANY)],
        out_specs=block,
        out_shape=jax.ShapeDtypeStruct(into.shape, into.dtype),
        input_output_aliases={1: 0},
        compiler_params=vmem(56),
        cost_estimate=pl.CostEstimate(
            flops=2**18, bytes_accessed=2**20, transcendentals=0
        ),
        name="fold",
    )(parts, into)


def project_kernel(x_ref, parts_ref, gain_ref, key_ref, value_ref, key_gain_ref, out_ref, text):
    h = pl.program_id(0)

    @pl.when(h == 0)
    def _():
        groups, depth, _ = parts_ref.shape
        each = depth // SLOT // 2
        count = x_ref.shape[0]
        columns = []
        for n in range(groups):
            for j in range(each):
                high = parts_ref[n, j * SLOT : (j + 1) * SLOT, :].astype(jnp.float32)
                low = parts_ref[n, (each + j) * SLOT : (each + j + 1) * SLOT, :]
                columns.append((high + low.astype(jnp.float32))[:count])
        x = x_ref[...].astype(jnp.float32) + jnp.concatenate(columns, axis=1)
        inverse = lax.rsqrt(jnp.mean(x * x, axis=-1, keepdims=True) + EPS)
        rows = x * inverse * gain_ref[...]
        spare = jnp.zeros((SLOT - count, x.shape[1]), jnp.float32)
        text[...] = jnp.concatenate([rows, spare], axis=0).astype(jnp.bfloat16)

    rows = text[...]
    keys = jnp.dot(rows, key_ref[...], preferred_element_type=jnp.float32)
    inverse = lax.rsqrt(jnp.mean(keys * keys, axis=-1, keepdims=True) + EPS)
    keys = (keys * inverse * key_gain_ref[...]).astype(jnp.bfloat16)
    values = jnp.dot(rows, value_ref[...], preferred_element_type=jnp.float32)
    values = values.astype(jnp.bfloat16)
    for n in range(out_ref.shape[0]):
        out_ref[n, :SLOT, :] = keys
        out_ref[n, SLOT:, :] = values


def project(x, parts, gain, key, value, key_gain, extra, copies):
    width, part = key.shape
    heads = part // HEAD
    weight = pl.BlockSpec((width, HEAD), lambda h: (0, h))
    return pl.pallas_call(
        project_kernel,
        grid=(heads,),
        in_specs=[
            pl.BlockSpec(x.shape, lambda h: (0, 0)),
            pl.BlockSpec((parts.shape[0], extra, HEAD), lambda h: (0, 0, 0)),
            pl.BlockSpec((1, width), lambda h: (0, 0)),
            weight,
            weight,
            pl.BlockSpec((1, HEAD), lambda h: (0, h)),
        ],
        out_specs=pl.BlockSpec((copies, 2 * SLOT, HEAD), lambda h: (0, h, 0)),
        out_shape=jax.ShapeDtypeStruct((copies, heads * 2 * SLOT, HEAD), jnp.bfloat16),
        scratch_shapes=[pltpu.VMEM((SLOT, width), jnp.bfloat16)],
        compiler_params=vmem(56),
        cost_estimate=pl.CostEstimate(
            flops=4 * SLOT * width * part, bytes_accessed=4 * width * part, transcendentals=0
        ),
        name="project",
    )(x, parts, gain[None, :], key, value, key_gain[None, :])


def attend_kernel(views, nq, nkv, ring, *refs):
    inputs, outs = refs[: len(views)], refs[len(views) : -5]
    q_s, k_s, v_s, o_s, sems = refs[-5:]
    blocks = q_s.shape[0] // nq
    copies = []
    counts = [0, 0]
    for ref, (kind, start) in zip(inputs, views):
        pieces = [ref] if len(ref.shape) == 3 else [ref.at[i] for i in range(ref.shape[0])]
        for piece in pieces:
            rows = pl.ds(counts[kind] * blocks, blocks)
            counts[kind] += 1
            targets = ((0, q_s),) if kind == 0 else ((0, k_s), (HEAD, v_s))
            for offset, scratch in targets:
                copies.append((piece.at[:, pl.ds(start + offset, HEAD), :], scratch.at[rows]))
    copies = [
        pltpu.make_async_copy(src, dst, sems.at[i]) for i, (src, dst) in enumerate(copies)
    ]
    for copy in copies:
        copy.start()
    for copy in copies:
        copy.wait()
    per_q = TILE // HEAD
    per_k = CHUNK // HEAD
    per_block = blocks // per_q

    def tile(t, _):
        q = q_s[pl.ds(t * per_q, per_q)].reshape(TILE, HEAD)
        acc = jnp.zeros((HEAD, TILE), jnp.float32)
        total = jnp.zeros((8, TILE), jnp.float32)
        for j in range(nkv * blocks // per_k):
            keys = k_s[j * per_k : (j + 1) * per_k].reshape(CHUNK, HEAD)
            s = lax.dot_general(
                keys, q, (((1,), (1,)), ((), ())), preferred_element_type=jnp.float32
            )
            p = jnp.exp2(s)
            total = total + jnp.sum(p.reshape(CHUNK // 8, 8, TILE), axis=0)
            values = jnp.concatenate(
                [v_s[j * per_k + i] for i in range(per_k)], axis=1
            )
            acc = acc + jnp.dot(
                values, p.astype(jnp.bfloat16), preferred_element_type=jnp.float32
            )
        row = jnp.sum(total, axis=0, keepdims=True)
        high = row.astype(jnp.bfloat16).astype(jnp.float32)
        words = jnp.concatenate(
            [jnp.broadcast_to(high, (8, TILE)), jnp.broadcast_to(row - high, (8, TILE))], axis=0
        )
        columns = pl.ds(pl.multiple_of((t % per_block) * TILE, TILE), TILE)
        slot = t // per_block
        if ring is not None:
            slot = ring(slot)
        o_s[slot, :HEAD, columns] = acc.astype(jnp.bfloat16)
        o_s[slot, HEAD:, columns] = words.astype(jnp.bfloat16)
        return 0

    lax.fori_loop(0, nq * per_block, tile, 0)
    if ring is not None:
        copies = [pltpu.make_async_copy(o_s, outs[0], sems.at[0])]
    else:
        copies = [
            pltpu.make_async_copy(o_s.at[i], ref, sems.at[i]) for i, ref in enumerate(outs)
        ]
    for copy in copies:
        copy.start()
    for copy in copies:
        copy.wait()


def attend(queries, pairs, ring=None):
    arrays = [array for array, _ in queries + pairs]
    views = [(0, start) for _, start in queries] + [(1, start) for _, start in pairs]
    nq, nkv = (sum(math.prod(a.shape[:-3]) for a, _ in part) for part in (queries, pairs))
    blocks = arrays[0].shape[-3]
    count = blocks * HEAD
    work = nq * nkv * count * count
    shapes = [jax.ShapeDtypeStruct((HEAD + EXTRA, count), jnp.bfloat16)] * nq
    if ring is not None:
        shapes = [jax.ShapeDtypeStruct((nq, HEAD + EXTRA, count), jnp.bfloat16)]
    return pl.pallas_call(
        lambda *refs: attend_kernel(views, nq, nkv, ring, *refs),
        in_specs=[pl.BlockSpec(memory_space=pl.ANY)] * len(arrays),
        out_specs=[pl.BlockSpec(memory_space=pl.ANY)] * len(shapes),
        out_shape=shapes,
        scratch_shapes=[
            pltpu.VMEM((nq * blocks, HEAD, HEAD), jnp.bfloat16),
            pltpu.VMEM((nkv * blocks, HEAD, HEAD), jnp.bfloat16),
            pltpu.VMEM((nkv * blocks, HEAD, HEAD), jnp.bfloat16),
            pltpu.VMEM((nq, HEAD + EXTRA, count), jnp.bfloat16),
            pltpu.SemaphoreType.DMA((nq + 2 * nkv,)),
        ],
        compiler_params=vmem(56),
        cost_estimate=pl.CostEstimate(
            flops=4 * HEAD * work, bytes_accessed=6 * 2**20, transcendentals=work
        ),
        name="attend",
    )(*arrays)


def merge_kernel(sizes, *refs):
    out_ref = refs[-1]
    refs = list(refs[:-1])
    for h, size in enumerate(sizes):
        group, refs = refs[:size], refs[size:]
        if size == 1:
            group = [group[0].at[i] for i in range(group[0].shape[0])]
        weighted = sum(ref[:HEAD, :].astype(jnp.float32) for ref in group)
        pieces = sum(ref[HEAD:, :].astype(jnp.float32) for ref in group)
        total = pieces[0:1] + pieces[8:9]
        out_ref[:, h * HEAD : (h + 1) * HEAD] = (weighted / total).T.astype(jnp.bfloat16)


def merge(results):
    heads = len(results)
    arrays = [array for group in results for array in group]
    sizes = [len(group) for group in results]
    count = arrays[0].shape[-1]
    step = 256
    specs = []
    for array in arrays:
        if array.ndim == 2:
            specs.append(pl.BlockSpec((array.shape[0], step), lambda i: (0, i)))
        else:
            specs.append(pl.BlockSpec(array.shape[:2] + (step,), lambda i: (0, 0, i)))
    return pl.pallas_call(
        lambda *refs: merge_kernel(sizes, *refs),
        grid=(count // step,),
        in_specs=specs,
        out_specs=pl.BlockSpec((step, heads * HEAD), lambda i: (i, 0)),
        out_shape=jax.ShapeDtypeStruct((count, heads * HEAD), jnp.bfloat16),
        compiler_params=vmem(56),
        cost_estimate=pl.CostEstimate(
            flops=count * heads * HEAD * 8, bytes_accessed=4 * 2**20, transcendentals=0
        ),
        name="merge",
    )(*arrays)


def cross_kernel(start, per, length_ref, c_ref, kv_ref, out_ref):
    live = length_ref[0]
    blocks = c_ref.shape[0]
    sources = kv_ref.shape[0]
    count = sources * SLOT
    tile = blocks * HEAD
    row = lax.broadcasted_iota(jnp.int32, (count, tile), 0)
    source, slot = row // SLOT, row % SLOT
    alive = (slot < per) & (source * per + slot < live)
    for h in range(kv_ref.shape[1] // (2 * SLOT)):
        at = 2 * h * SLOT
        keys = kv_ref[:, at : at + SLOT, :].reshape(count, HEAD)
        values = kv_ref[:, at + SLOT : at + 2 * SLOT, :].reshape(count, HEAD)
        values = values.astype(jnp.float32).T.astype(jnp.bfloat16)
        first = start + h * HEAD
        q = c_ref[:, first : first + HEAD, :].reshape(tile, HEAD)
        s = lax.dot_general(
            keys, q, (((1,), (1,)), ((), ())), preferred_element_type=jnp.float32
        )
        p = jnp.where(alive, jnp.exp2(s), 0.0)
        total = jnp.sum(p, axis=0, keepdims=True)
        weighted = jnp.dot(values, p.astype(jnp.bfloat16), preferred_element_type=jnp.float32)
        out_ref[:, h * HEAD : (h + 1) * HEAD] = (weighted / total).T.astype(jnp.bfloat16)


def cross(lengths, c, start, kv, per):
    blocks, depth, _ = c.shape
    step = 4
    heads = kv.shape[1] // (2 * SLOT)
    return pl.pallas_call(
        lambda *refs: cross_kernel(start, per, *refs),
        grid=(blocks // step,),
        in_specs=[
            pl.BlockSpec(memory_space=pltpu.SMEM),
            pl.BlockSpec((step, depth, HEAD), lambda i: (i, 0, 0)),
            pl.BlockSpec(kv.shape, lambda i: (0, 0, 0)),
        ],
        out_specs=pl.BlockSpec((step * HEAD, heads * HEAD), lambda i: (i, 0)),
        out_shape=jax.ShapeDtypeStruct((blocks * HEAD, heads * HEAD), jnp.bfloat16),
        compiler_params=vmem(56),
        cost_estimate=pl.CostEstimate(
            flops=4 * HEAD * heads * blocks * HEAD * kv.shape[0] * SLOT,
            bytes_accessed=3 * 2**20,
            transcendentals=heads * blocks * HEAD * kv.shape[0] * SLOT,
        ),
        name="cross",
    )(lengths, c, kv)


def spot(hi, z, core):
    return hi * 8 + z * 2 + core


def wide_pairs(move):
    places = [(hi, z, core) for hi in range(2) for z in range(4) for core in range(2)]
    return [(spot(*place), spot(*move(*place))) for place in places]


UP = wide_pairs(lambda hi, z, core: (hi, (z + 1) % 4, core))
DOWN = wide_pairs(lambda hi, z, core: (hi, (z + 3) % 4, core))
ACROSS = wide_pairs(lambda hi, z, core: (hi, (z + 2) % 4, core))
OTHER_X = wide_pairs(lambda hi, z, core: (1 - hi, z, core))
OTHER_CORE = wide_pairs(lambda hi, z, core: (hi, z, 1 - core))
ALONG_Z = [[spot(hi, z, core) for z in range(4)] for hi in range(2) for core in range(2)]
ALONG_X = [[spot(hi, z, core) for hi in range(2) for core in range(2)] for z in range(4)]


def send(array, pairs):
    return lax.ppermute(array, "wide", pairs)


def collect(array, groups):
    return lax.all_gather(array, "wide", axis=0, axis_index_groups=groups)


def give_back(parts):
    own, below, above, across = parts
    return [own, send(below, DOWN), send(above, UP), send(across, ACROSS)]


def trade_back(parts):
    return lax.all_to_all(
        parts, "wide", split_axis=0, concat_axis=0, axis_index_groups=ALONG_Z, tiled=True
    )


def from_ring(block):
    z = lax.axis_index("wide") // 2 % 4
    shift = jnp.where(block == 1, 3, jnp.where(block == 2, 1, jnp.where(block == 3, 2, 0)))
    return (z + shift) % 4


def around(array):
    return [send(array, UP), send(array, DOWN), send(array, ACROSS)]


def after(arrays):
    return lax.optimization_barrier(arrays)


def trade(array):
    return lax.all_to_all(array, "narrow", split_axis=0, concat_axis=0, tiled=True)


def body(
    prompt_states,
    prompt_lengths,
    feed_gain,
    gate_weight,
    up_weight,
    down_weight,
    final_gain,
    key_weight,
    value_weight,
    prompt_key_gain,
    latent_queries,
    latent_keys,
    latent_values,
    cross_queries,
    query_gain,
    key_gain,
    cross_query_gain,
):
    groups = latent_queries.shape[1] // key_weight.shape[1]
    per, width = prompt_states.shape
    extra = width // groups // HEAD * SLOT * 2
    heads = key_weight.shape[1] // HEAD
    each = 3 * HEAD
    arrays = (latent_queries, latent_keys, latent_values, cross_queries)
    gains = (query_gain, key_gain, cross_query_gain)

    def split(traded, base):
        pair = traded[:, base : base + 2 * HEAD]
        return traded[:, base + 2 * HEAD : base + 3 * HEAD], pair

    early = {"heads": [(0, 0, 0), (1, 0, each)], "crossed": []}
    late = {
        "heads": [(2, 0, extra)],
        "crossed": [(h, 0, extra + (3 + h) * HEAD) for h in range(heads)],
    }

    def plain(queries, pairs):
        return [(a, 0) for a in queries], [(a, 0) for a in pairs]

    (packed,) = pack(arrays, gains, groups, heads, early, [2 * each])
    traded = trade(packed)
    (final,) = pack(arrays, gains, groups, heads, late, [extra + 2 * each])
    pieces = feed(prompt_states, feed_gain, gate_weight, up_weight, down_weight, groups, extra)
    traded, pieces, final = after((traded, pieces, final))
    final = fold(trade(pieces), final)

    query0, pair0 = split(traded, 0)
    pair_x0 = send(pair0, OTHER_X)
    queries0 = [query0] + around(query0)
    pairs0 = [pair0, send(pair0, OTHER_CORE)]
    query1, pair1 = split(traded, each)
    pair_x1 = send(pair1, OTHER_X)
    queries1 = [query1] + around(query1)
    pairs1 = [pair1, send(pair1, OTHER_CORE)]
    pair_x0, queries0, final = after((pair_x0, queries0, final))
    final = trade(final)
    pairs0 += [pair_x0, send(pair_x0, OTHER_CORE)]
    part0 = attend(*plain(queries0, pairs0), from_ring)

    final, part0, queries1, pair_x1 = after((final, part0, queries1, pair_x1))
    pairs1 += [pair_x1, send(pair_x1, OTHER_CORE)]
    query2, pair2 = split(final, extra)
    pair_x2 = send(pair2, OTHER_X)
    queries2 = [query2] + around(query2)
    pairs2 = [pair2, send(pair2, OTHER_CORE)]
    result0 = trade_back(part0[0])
    part1 = attend(*plain(queries1, pairs1))

    tied = (part1, queries2, pair_x2, pairs2, result0, final)
    part1, queries2, pair_x2, pairs2, result0, folded = after(tied)
    pairs2 += [pair_x2, send(pair_x2, OTHER_CORE)]
    result1 = give_back(part1)
    prompt_pair = project(
        prompt_states,
        folded,
        final_gain,
        key_weight,
        value_weight,
        prompt_key_gain,
        extra,
        lax.axis_size("wide"),
    )
    prompt_pair = lax.all_to_all(prompt_pair, "wide", split_axis=0, concat_axis=0, tiled=True)
    others = attend(*plain(queries2[1:], pairs2))
    result1, others, prompt_pair = after((result1, others, prompt_pair))
    below, above, across = others
    result2 = [send(below, DOWN), send(above, UP), send(across, ACROSS)]
    result2 += attend(*plain(queries2[:1], pairs2))
    results = [[result0], result1, result2]
    cross_out = cross(prompt_lengths, final, extra + each, prompt_pair, per)
    results, cross_out = after((results, cross_out))
    self_out = merge(results)
    return (self_out, cross_out)


def solution(mesh):
    rows = P(("wide", "narrow"), None)
    return jax.shard_map(
        body,
        mesh=mesh,
        in_specs=(
            P("wide", None),
            P(),
            P(),
            P(None, "narrow"),
            P(None, "narrow"),
            P("narrow", None),
            P(),
            P(None, "narrow"),
            P(None, "narrow"),
            P("narrow"),
            rows,
            rows,
            rows,
            rows,
            P(),
            P(),
            P(),
        ),
        out_specs=(P("wide", "narrow"), P("wide", "narrow")),
        check_vma=False,
    )
```

```python
import math

import jax
import jax.numpy as jnp
from jax import lax
from jax.experimental import pallas as pl
from jax.experimental.pallas import tpu as pltpu
from jax.sharding import PartitionSpec as P

HEAD = 128
EPS = 1e-06
SCALE = math.log2(math.e) / math.sqrt(HEAD)
TILE = 512
CHUNK = 2048
EXTRA = 16
SLOT = 32


def vmem(mib):
    return pltpu.CompilerParams(vmem_limit_bytes=mib * 2**20)


def normed(ref, gain_ref, at, factor):
    x = ref[:, at].astype(jnp.float32)
    inverse = lax.rsqrt(jnp.mean(x * x, axis=-1, keepdims=True) + EPS)
    return (x * inverse * (gain_ref[:, at] * factor)).astype(jnp.bfloat16)


def pack_kernel(heads, plan, q_ref, k_ref, v_ref, qg_ref, kg_ref, *rest):
    groups = rest[-1].shape[0]
    outs = rest[2:] if plan["crossed"] else rest

    def group(n, _):
        for h, out, pair, query in plan["heads"]:
            at = pl.ds(pl.multiple_of((n * heads + h) * HEAD, HEAD), HEAD)
            ref = outs[out]
            ref[n, pair : pair + HEAD, :] = normed(k_ref, kg_ref, at, 1.0)
            ref[n, pair + HEAD : pair + 2 * HEAD, :] = (
                v_ref[:, at].astype(jnp.float32).T.astype(jnp.bfloat16)
            )
            ref[n, query : query + HEAD, :] = normed(q_ref, qg_ref, at, SCALE)
        for h, out, base in plan["crossed"]:
            at = pl.ds(pl.multiple_of((n * heads + h) * HEAD, HEAD), HEAD)
            outs[out][n, base : base + HEAD, :] = normed(rest[0], rest[1], at, SCALE)
        return 0

    lax.fori_loop(0, groups, group, 0)


def pack(arrays, gains, groups, heads, plan, depths):
    whole = pl.BlockSpec(memory_space=pltpu.VMEM)
    operands = list(arrays[:3]) + [gain[None, :] for gain in gains[:2]]
    if plan["crossed"]:
        operands += [arrays[3], gains[2][None, :]]
    units = 3 * len(plan["heads"]) + len(plan["crossed"])
    return pl.pallas_call(
        lambda *refs: pack_kernel(heads, plan, *refs),
        in_specs=[whole] * len(operands),
        out_specs=[whole] * len(depths),
        out_shape=[
            jax.ShapeDtypeStruct((groups, depth, HEAD), jnp.bfloat16) for depth in depths
        ],
        compiler_params=vmem(56),
        cost_estimate=pl.CostEstimate(
            flops=8 * arrays[0].size, bytes_accessed=units * 2**20, transcendentals=0
        ),
        name="pack",
    )(*operands)


def words(block):
    high = block.astype(jnp.bfloat16)
    return high, (block - high.astype(jnp.float32)).astype(jnp.bfloat16)


def feed_kernel(x_ref, gain_ref, gate_ref, up_ref, down_ref, out_ref, rows_ref, total):
    step = pl.program_id(0)

    @pl.when(step == 0)
    def _():
        x = x_ref[...].astype(jnp.float32)
        inverse = lax.rsqrt(jnp.mean(x * x, axis=-1, keepdims=True) + EPS)
        rows = x * inverse * gain_ref[...]
        spare = jnp.zeros((SLOT - x.shape[0], x.shape[1]), jnp.float32)
        rows_ref[...] = jnp.concatenate([rows, spare], axis=0).astype(jnp.bfloat16)
        total[...] = jnp.zeros_like(total)

    rows = rows_ref[...]
    gate = jnp.dot(rows, gate_ref[...], preferred_element_type=jnp.float32)
    upward = jnp.dot(rows, up_ref[...], preferred_element_type=jnp.float32)
    hidden = (jax.nn.gelu(gate, approximate=True) * upward).astype(jnp.bfloat16)
    total[...] += jnp.dot(hidden, down_ref[...], preferred_element_type=jnp.float32)

    @pl.when(step == pl.num_programs(0) - 1)
    def _():
        groups = out_ref.shape[0]
        each = total.shape[1] // groups // HEAD
        for n in range(groups):
            for j in range(each):
                at = (n * each + j) * HEAD
                high, low = words(total[:, at : at + HEAD])
                out_ref[n, j * SLOT : (j + 1) * SLOT, :] = high
                out_ref[n, (each + j) * SLOT : (each + j + 1) * SLOT, :] = low


def feed(x, gain, gate, up, down, groups, extra):
    width, hidden = gate.shape
    tile = HEAD
    return pl.pallas_call(
        feed_kernel,
        grid=(hidden // tile,),
        in_specs=[
            pl.BlockSpec(x.shape, lambda i: (0, 0)),
            pl.BlockSpec((1, width), lambda i: (0, 0)),
            pl.BlockSpec((width, tile), lambda i: (0, i)),
            pl.BlockSpec((width, tile), lambda i: (0, i)),
            pl.BlockSpec((tile, width), lambda i: (i, 0)),
        ],
        out_specs=pl.BlockSpec((groups, extra, HEAD), lambda i: (0, 0, 0)),
        out_shape=jax.ShapeDtypeStruct((groups, extra, HEAD), jnp.bfloat16),
        scratch_shapes=[
            pltpu.VMEM((SLOT, width), jnp.bfloat16),
            pltpu.VMEM((SLOT, width), jnp.float32),
        ],
        compiler_params=vmem(56),
        cost_estimate=pl.CostEstimate(
            flops=6 * SLOT * width * hidden,
            bytes_accessed=6 * width * hidden,
            transcendentals=SLOT * hidden,
        ),
        name="feed",
    )(x, gain[None, :], gate, up, down)


def fold_kernel(parts_ref, _, out_ref):
    groups, depth, _ = parts_ref.shape
    half = depth // 2
    total = jnp.zeros((half, HEAD), jnp.float32)
    for n in range(groups):
        total = total + parts_ref[n, :half, :].astype(jnp.float32)
        total = total + parts_ref[n, half:, :].astype(jnp.float32)
    high, low = words(total)
    for n in range(groups):
        out_ref[n, :half, :] = high
        out_ref[n, half:, :] = low


def fold(parts, into):
    block = pl.BlockSpec(parts.shape, lambda i: (0, 0, 0))
    return pl.pallas_call(
        fold_kernel,
        grid=(1,),
        in_specs=[block, pl.BlockSpec(memory_space=pl.ANY)],
        out_specs=block,
        out_shape=jax.ShapeDtypeStruct(into.shape, into.dtype),
        input_output_aliases={1: 0},
        compiler_params=vmem(56),
        cost_estimate=pl.CostEstimate(
            flops=2**18, bytes_accessed=2**20, transcendentals=0
        ),
        name="fold",
    )(parts, into)


def project_kernel(x_ref, parts_ref, gain_ref, key_ref, value_ref, key_gain_ref, out_ref, text):
    h = pl.program_id(0)

    @pl.when(h == 0)
    def _():
        groups, depth, _ = parts_ref.shape
        each = depth // SLOT // 2
        count = x_ref.shape[0]
        columns = []
        for n in range(groups):
            for j in range(each):
                high = parts_ref[n, j * SLOT : (j + 1) * SLOT, :].astype(jnp.float32)
                low = parts_ref[n, (each + j) * SLOT : (each + j + 1) * SLOT, :]
                columns.append((high + low.astype(jnp.float32))[:count])
        x = x_ref[...].astype(jnp.float32) + jnp.concatenate(columns, axis=1)
        inverse = lax.rsqrt(jnp.mean(x * x, axis=-1, keepdims=True) + EPS)
        rows = x * inverse * gain_ref[...]
        spare = jnp.zeros((SLOT - count, x.shape[1]), jnp.float32)
        text[...] = jnp.concatenate([rows, spare], axis=0).astype(jnp.bfloat16)

    rows = text[...]
    keys = jnp.dot(rows, key_ref[...], preferred_element_type=jnp.float32)
    inverse = lax.rsqrt(jnp.mean(keys * keys, axis=-1, keepdims=True) + EPS)
    keys = (keys * inverse * key_gain_ref[...]).astype(jnp.bfloat16)
    values = jnp.dot(rows, value_ref[...], preferred_element_type=jnp.float32)
    values = values.astype(jnp.bfloat16)
    for n in range(out_ref.shape[0]):
        out_ref[n, :SLOT, :] = keys
        out_ref[n, SLOT:, :] = values


def project(x, parts, gain, key, value, key_gain, extra, copies):
    width, part = key.shape
    heads = part // HEAD
    weight = pl.BlockSpec((width, HEAD), lambda h: (0, h))
    return pl.pallas_call(
        project_kernel,
        grid=(heads,),
        in_specs=[
            pl.BlockSpec(x.shape, lambda h: (0, 0)),
            pl.BlockSpec((parts.shape[0], extra, HEAD), lambda h: (0, 0, 0)),
            pl.BlockSpec((1, width), lambda h: (0, 0)),
            weight,
            weight,
            pl.BlockSpec((1, HEAD), lambda h: (0, h)),
        ],
        out_specs=pl.BlockSpec((copies, 2 * SLOT, HEAD), lambda h: (0, h, 0)),
        out_shape=jax.ShapeDtypeStruct((copies, heads * 2 * SLOT, HEAD), jnp.bfloat16),
        scratch_shapes=[pltpu.VMEM((SLOT, width), jnp.bfloat16)],
        compiler_params=vmem(56),
        cost_estimate=pl.CostEstimate(
            flops=4 * SLOT * width * part, bytes_accessed=4 * width * part, transcendentals=0
        ),
        name="project",
    )(x, parts, gain[None, :], key, value, key_gain[None, :])


def attend_kernel(views, nq, nkv, ring, *refs):
    inputs, outs = refs[: len(views)], refs[len(views) : -5]
    q_s, k_s, v_s, o_s, sems = refs[-5:]
    blocks = q_s.shape[0] // nq
    copies = []
    counts = [0, 0]
    for ref, (kind, start) in zip(inputs, views):
        pieces = [ref] if len(ref.shape) == 3 else [ref.at[i] for i in range(ref.shape[0])]
        for piece in pieces:
            rows = pl.ds(counts[kind] * blocks, blocks)
            counts[kind] += 1
            targets = ((0, q_s),) if kind == 0 else ((0, k_s), (HEAD, v_s))
            for offset, scratch in targets:
                copies.append((piece.at[:, pl.ds(start + offset, HEAD), :], scratch.at[rows]))
    copies = [
        pltpu.make_async_copy(src, dst, sems.at[i]) for i, (src, dst) in enumerate(copies)
    ]
    for copy in copies:
        copy.start()
    for copy in copies:
        copy.wait()
    per_q = TILE // HEAD
    per_k = CHUNK // HEAD
    per_block = blocks // per_q

    def tile(t, _):
        q = q_s[pl.ds(t * per_q, per_q)].reshape(TILE, HEAD)
        acc = jnp.zeros((HEAD, TILE), jnp.float32)
        total = jnp.zeros((8, TILE), jnp.float32)
        for j in range(nkv * blocks // per_k):
            keys = k_s[j * per_k : (j + 1) * per_k].reshape(CHUNK, HEAD)
            s = lax.dot_general(
                keys, q, (((1,), (1,)), ((), ())), preferred_element_type=jnp.float32
            )
            p = jnp.exp2(s)
            total = total + jnp.sum(p.reshape(CHUNK // 8, 8, TILE), axis=0)
            values = jnp.concatenate(
                [v_s[j * per_k + i] for i in range(per_k)], axis=1
            )
            acc = acc + jnp.dot(
                values, p.astype(jnp.bfloat16), preferred_element_type=jnp.float32
            )
        row = jnp.sum(total, axis=0, keepdims=True)
        high = row.astype(jnp.bfloat16).astype(jnp.float32)
        words = jnp.concatenate(
            [jnp.broadcast_to(high, (8, TILE)), jnp.broadcast_to(row - high, (8, TILE))], axis=0
        )
        columns = pl.ds(pl.multiple_of((t % per_block) * TILE, TILE), TILE)
        slot = t // per_block
        if ring is not None:
            slot = ring(slot)
        o_s[slot, :HEAD, columns] = acc.astype(jnp.bfloat16)
        o_s[slot, HEAD:, columns] = words.astype(jnp.bfloat16)
        return 0

    lax.fori_loop(0, nq * per_block, tile, 0)
    if ring is not None:
        copies = [pltpu.make_async_copy(o_s, outs[0], sems.at[0])]
    else:
        copies = [
            pltpu.make_async_copy(o_s.at[i], ref, sems.at[i]) for i, ref in enumerate(outs)
        ]
    for copy in copies:
        copy.start()
    for copy in copies:
        copy.wait()


def attend(queries, pairs, ring=None):
    arrays = [array for array, _ in queries + pairs]
    views = [(0, start) for _, start in queries] + [(1, start) for _, start in pairs]
    nq, nkv = (sum(math.prod(a.shape[:-3]) for a, _ in part) for part in (queries, pairs))
    blocks = arrays[0].shape[-3]
    count = blocks * HEAD
    work = nq * nkv * count * count
    shapes = [jax.ShapeDtypeStruct((HEAD + EXTRA, count), jnp.bfloat16)] * nq
    if ring is not None:
        shapes = [jax.ShapeDtypeStruct((nq, HEAD + EXTRA, count), jnp.bfloat16)]
    return pl.pallas_call(
        lambda *refs: attend_kernel(views, nq, nkv, ring, *refs),
        in_specs=[pl.BlockSpec(memory_space=pl.ANY)] * len(arrays),
        out_specs=[pl.BlockSpec(memory_space=pl.ANY)] * len(shapes),
        out_shape=shapes,
        scratch_shapes=[
            pltpu.VMEM((nq * blocks, HEAD, HEAD), jnp.bfloat16),
            pltpu.VMEM((nkv * blocks, HEAD, HEAD), jnp.bfloat16),
            pltpu.VMEM((nkv * blocks, HEAD, HEAD), jnp.bfloat16),
            pltpu.VMEM((nq, HEAD + EXTRA, count), jnp.bfloat16),
            pltpu.SemaphoreType.DMA((nq + 2 * nkv,)),
        ],
        compiler_params=vmem(56),
        cost_estimate=pl.CostEstimate(
            flops=4 * HEAD * work, bytes_accessed=6 * 2**20, transcendentals=work
        ),
        name="attend",
    )(*arrays)


def merge_kernel(sizes, *refs):
    out_ref = refs[-1]
    refs = list(refs[: sum(sizes)])
    for h, size in enumerate(sizes):
        group, refs = refs[:size], refs[size:]
        if size == 1:
            group = [group[0].at[i] for i in range(group[0].shape[0])]
        weighted = sum(ref[:HEAD, :].astype(jnp.float32) for ref in group)
        pieces = sum(ref[HEAD:, :].astype(jnp.float32) for ref in group)
        total = pieces[0:1] + pieces[8:9]
        out_ref[:, h * HEAD : (h + 1) * HEAD] = (weighted / total).T.astype(jnp.bfloat16)


def merge(results, width, column, into=None):
    heads = len(results)
    arrays = [array for group in results for array in group]
    sizes = [len(group) for group in results]
    count = arrays[0].shape[-1]
    step = 256
    specs = []
    for array in arrays:
        if array.ndim == 2:
            specs.append(pl.BlockSpec((array.shape[0], step), lambda i: (0, i)))
        else:
            specs.append(pl.BlockSpec(array.shape[:2] + (step,), lambda i: (0, 0, i)))
    aliases = {}
    if into is not None:
        aliases = {len(arrays): 0}
        arrays.append(into)
        specs.append(pl.BlockSpec(memory_space=pl.ANY))
    return pl.pallas_call(
        lambda *refs: merge_kernel(sizes, *refs),
        grid=(count // step,),
        in_specs=specs,
        out_specs=pl.BlockSpec((step, heads * HEAD), lambda i: (i, column)),
        out_shape=jax.ShapeDtypeStruct((count, width), jnp.bfloat16),
        input_output_aliases=aliases,
        compiler_params=vmem(56),
        cost_estimate=pl.CostEstimate(
            flops=count * heads * HEAD * 8, bytes_accessed=heads * 2**21, transcendentals=0
        ),
        name="merge",
    )(*arrays)


def cross_kernel(start, per, length_ref, c_ref, kv_ref, out_ref):
    live = length_ref[0]
    blocks = c_ref.shape[0]
    sources = kv_ref.shape[0]
    count = sources * SLOT
    tile = blocks * HEAD
    row = lax.broadcasted_iota(jnp.int32, (count, tile), 0)
    source, slot = row // SLOT, row % SLOT
    alive = (slot < per) & (source * per + slot < live)
    for h in range(kv_ref.shape[1] // (2 * SLOT)):
        at = 2 * h * SLOT
        keys = kv_ref[:, at : at + SLOT, :].reshape(count, HEAD)
        values = kv_ref[:, at + SLOT : at + 2 * SLOT, :].reshape(count, HEAD)
        values = values.astype(jnp.float32).T.astype(jnp.bfloat16)
        first = start + h * HEAD
        q = c_ref[:, first : first + HEAD, :].reshape(tile, HEAD)
        s = lax.dot_general(
            keys, q, (((1,), (1,)), ((), ())), preferred_element_type=jnp.float32
        )
        p = jnp.where(alive, jnp.exp2(s), 0.0)
        total = jnp.sum(p, axis=0, keepdims=True)
        weighted = jnp.dot(values, p.astype(jnp.bfloat16), preferred_element_type=jnp.float32)
        out_ref[:, h * HEAD : (h + 1) * HEAD] = (weighted / total).T.astype(jnp.bfloat16)


def cross(lengths, c, start, kv, per):
    blocks, depth, _ = c.shape
    step = 4
    heads = kv.shape[1] // (2 * SLOT)
    return pl.pallas_call(
        lambda *refs: cross_kernel(start, per, *refs),
        grid=(blocks // step,),
        in_specs=[
            pl.BlockSpec(memory_space=pltpu.SMEM),
            pl.BlockSpec((step, depth, HEAD), lambda i: (i, 0, 0)),
            pl.BlockSpec(kv.shape, lambda i: (0, 0, 0)),
        ],
        out_specs=pl.BlockSpec((step * HEAD, heads * HEAD), lambda i: (i, 0)),
        out_shape=jax.ShapeDtypeStruct((blocks * HEAD, heads * HEAD), jnp.bfloat16),
        compiler_params=vmem(56),
        cost_estimate=pl.CostEstimate(
            flops=4 * HEAD * heads * blocks * HEAD * kv.shape[0] * SLOT,
            bytes_accessed=3 * 2**20,
            transcendentals=heads * blocks * HEAD * kv.shape[0] * SLOT,
        ),
        name="cross",
    )(lengths, c, kv)


def spot(hi, z, core):
    return hi * 8 + z * 2 + core


def wide_pairs(move):
    places = [(hi, z, core) for hi in range(2) for z in range(4) for core in range(2)]
    return [(spot(*place), spot(*move(*place))) for place in places]


UP = wide_pairs(lambda hi, z, core: (hi, (z + 1) % 4, core))
DOWN = wide_pairs(lambda hi, z, core: (hi, (z + 3) % 4, core))
ACROSS = wide_pairs(lambda hi, z, core: (hi, (z + 2) % 4, core))
OTHER_X = wide_pairs(lambda hi, z, core: (1 - hi, z, core))
OTHER_CORE = wide_pairs(lambda hi, z, core: (hi, z, 1 - core))
ALONG_Z = [[spot(hi, z, core) for z in range(4)] for hi in range(2) for core in range(2)]
ALONG_X = [[spot(hi, z, core) for hi in range(2) for core in range(2)] for z in range(4)]


def send(array, pairs):
    return lax.ppermute(array, "wide", pairs)


def collect(array, groups):
    return lax.all_gather(array, "wide", axis=0, axis_index_groups=groups)


def give_back(parts):
    own, below, above, across = parts
    return [own, send(below, DOWN), send(above, UP), send(across, ACROSS)]


def trade_back(parts):
    return lax.all_to_all(
        parts, "wide", split_axis=0, concat_axis=0, axis_index_groups=ALONG_Z, tiled=True
    )


def from_ring(block):
    z = lax.axis_index("wide") // 2 % 4
    shift = jnp.where(block == 1, 3, jnp.where(block == 2, 1, jnp.where(block == 3, 2, 0)))
    return (z + shift) % 4


def around(array):
    return [send(array, UP), send(array, DOWN), send(array, ACROSS)]


def after(arrays):
    return lax.optimization_barrier(arrays)


def trade(array):
    return lax.all_to_all(array, "narrow", split_axis=0, concat_axis=0, tiled=True)


def body(
    prompt_states,
    prompt_lengths,
    feed_gain,
    gate_weight,
    up_weight,
    down_weight,
    final_gain,
    key_weight,
    value_weight,
    prompt_key_gain,
    latent_queries,
    latent_keys,
    latent_values,
    cross_queries,
    query_gain,
    key_gain,
    cross_query_gain,
):
    groups = latent_queries.shape[1] // key_weight.shape[1]
    per, width = prompt_states.shape
    extra = width // groups // HEAD * SLOT * 2
    heads = key_weight.shape[1] // HEAD
    each = 3 * HEAD
    last = heads - 1
    arrays = (latent_queries, latent_keys, latent_values, cross_queries)
    gains = (query_gain, key_gain, cross_query_gain)

    def split(traded, base, count):
        middle, end = base + 2 * count * HEAD, base + 3 * count * HEAD
        return traded[:, middle:end], traded[:, base:middle]

    early = {
        "heads": [(0, 0, 0, 4 * HEAD), (1, 0, 2 * HEAD, 5 * HEAD)],
        "crossed": [],
    }
    late = {
        "heads": [(2, 0, extra, extra + 2 * HEAD)],
        "crossed": [(h, 0, extra + (3 + h) * HEAD) for h in range(heads)],
    }

    def views(queries, pairs, h=0):
        return [(a, h * HEAD) for a in queries], [(a, 2 * h * HEAD) for a in pairs]

    (packed,) = pack(arrays, gains, groups, heads, early, [2 * each])
    traded = trade(packed)
    (final,) = pack(arrays, gains, groups, heads, late, [extra + 2 * each])
    pieces = feed(prompt_states, feed_gain, gate_weight, up_weight, down_weight, groups, extra)
    traded, pieces, final = after((traded, pieces, final))
    query, pair = split(traded, 0, 2)
    pair_x = send(pair, OTHER_X)
    queries = [query] + around(query)
    pairs = [pair, send(pair, OTHER_CORE)]
    final = fold(trade(pieces), final)
    pair_x, queries, token = after((pair_x, queries, final[:1, :16]))
    final = trade(final)
    pairs += [pair_x, send(pair_x, OTHER_CORE)]
    part0 = attend(*views(queries, pairs), from_ring)
    final, part0 = after((final, part0))
    query2, pair2 = split(final, extra, 1)
    pair_x2 = send(pair2, OTHER_X)
    queries2 = [query2] + around(query2)
    pairs2 = [pair2, send(pair2, OTHER_CORE)]
    result0 = trade_back(part0[0])
    part1 = attend(*views(queries, pairs, 1))

    tied = (part1, queries2, pair_x2, pairs2, result0, final)
    part1, queries2, pair_x2, pairs2, result0, folded = after(tied)
    pairs2 += [pair_x2, send(pair_x2, OTHER_CORE)]
    result1 = give_back(part1)
    prompt_pair = project(
        prompt_states,
        folded,
        final_gain,
        key_weight,
        value_weight,
        prompt_key_gain,
        extra,
        lax.axis_size("wide"),
    )
    prompt_pair = lax.all_to_all(prompt_pair, "wide", split_axis=0, concat_axis=0, tiled=True)
    others = attend(*views(queries2[1:], pairs2))
    result1[:3], others, prompt_pair = after((result1[:3], others, prompt_pair))
    below, above, across = others
    result2 = [send(below, DOWN), send(above, UP), send(across, ACROSS)]
    result2 += attend(*views(queries2[:1], pairs2))
    cross_out = cross(prompt_lengths, final, extra + each, prompt_pair, per)
    self_out = merge([[result0], result1], heads * HEAD, 0)
    result2, cross_out, self_out = after((result2, cross_out, self_out))
    self_out = merge([result2], heads * HEAD, last, self_out)
    return (self_out, cross_out)


def solution(mesh):
    rows = P(("wide", "narrow"), None)
    return jax.shard_map(
        body,
        mesh=mesh,
        in_specs=(
            P("wide", None),
            P(),
            P(),
            P(None, "narrow"),
            P(None, "narrow"),
            P("narrow", None),
            P(),
            P(None, "narrow"),
            P(None, "narrow"),
            P("narrow"),
            rows,
            rows,
            rows,
            rows,
            P(),
            P(),
            P(),
        ),
        out_specs=(P("wide", "narrow"), P("wide", "narrow")),
        check_vma=False,
    )
```

```python
import math

import jax
import jax.numpy as jnp
from jax import lax
from jax.experimental import pallas as pl
from jax.experimental.pallas import tpu as pltpu
from jax.sharding import PartitionSpec as P

HEAD = 128
EPS = 1e-06
SCALE = math.log2(math.e) / math.sqrt(HEAD)
TILE = 512
CHUNK = 2048
EXTRA = 16
SLOT = 32


def vmem(mib):
    return pltpu.CompilerParams(vmem_limit_bytes=mib * 2**20)


def normed(ref, gain_ref, at, factor):
    x = ref[:, at].astype(jnp.float32)
    inverse = lax.rsqrt(jnp.mean(x * x, axis=-1, keepdims=True) + EPS)
    return (x * inverse * (gain_ref[:, at] * factor)).astype(jnp.bfloat16)


def pack_kernel(heads, plan, q_ref, k_ref, v_ref, qg_ref, kg_ref, *rest):
    groups = rest[-1].shape[0]
    outs = rest[2:] if plan["crossed"] else rest

    def group(n, _):
        for h, out, pair, query in plan["heads"]:
            at = pl.ds(pl.multiple_of((n * heads + h) * HEAD, HEAD), HEAD)
            ref = outs[out]
            ref[n, pair : pair + HEAD, :] = normed(k_ref, kg_ref, at, 1.0)
            ref[n, pair + HEAD : pair + 2 * HEAD, :] = (
                v_ref[:, at].astype(jnp.float32).T.astype(jnp.bfloat16)
            )
            ref[n, query : query + HEAD, :] = normed(q_ref, qg_ref, at, SCALE)
        for h, out, base in plan["crossed"]:
            at = pl.ds(pl.multiple_of((n * heads + h) * HEAD, HEAD), HEAD)
            outs[out][n, base : base + HEAD, :] = normed(rest[0], rest[1], at, SCALE)
        return 0

    lax.fori_loop(0, groups, group, 0)


def pack(arrays, gains, groups, heads, plan, depths):
    whole = pl.BlockSpec(memory_space=pltpu.VMEM)
    operands = list(arrays[:3]) + [gain[None, :] for gain in gains[:2]]
    if plan["crossed"]:
        operands += [arrays[3], gains[2][None, :]]
    units = 3 * len(plan["heads"]) + len(plan["crossed"])
    return pl.pallas_call(
        lambda *refs: pack_kernel(heads, plan, *refs),
        in_specs=[whole] * len(operands),
        out_specs=[whole] * len(depths),
        out_shape=[
            jax.ShapeDtypeStruct((groups, depth, HEAD), jnp.bfloat16) for depth in depths
        ],
        compiler_params=vmem(56),
        cost_estimate=pl.CostEstimate(
            flops=8 * arrays[0].size, bytes_accessed=units * 2**20, transcendentals=0
        ),
        name="pack",
    )(*operands)


def words(block):
    high = block.astype(jnp.bfloat16)
    return high, (block - high.astype(jnp.float32)).astype(jnp.bfloat16)


def feed_kernel(x_ref, gain_ref, gate_ref, up_ref, down_ref, out_ref, rows_ref, total):
    step = pl.program_id(0)

    @pl.when(step == 0)
    def _():
        x = x_ref[...].astype(jnp.float32)
        inverse = lax.rsqrt(jnp.mean(x * x, axis=-1, keepdims=True) + EPS)
        rows = x * inverse * gain_ref[...]
        spare = jnp.zeros((SLOT - x.shape[0], x.shape[1]), jnp.float32)
        rows_ref[...] = jnp.concatenate([rows, spare], axis=0).astype(jnp.bfloat16)
        total[...] = jnp.zeros_like(total)

    rows = rows_ref[...]
    gate = jnp.dot(rows, gate_ref[...], preferred_element_type=jnp.float32)
    upward = jnp.dot(rows, up_ref[...], preferred_element_type=jnp.float32)
    hidden = (jax.nn.gelu(gate, approximate=True) * upward).astype(jnp.bfloat16)
    total[...] += jnp.dot(hidden, down_ref[...], preferred_element_type=jnp.float32)

    @pl.when(step == pl.num_programs(0) - 1)
    def _():
        groups = out_ref.shape[0]
        each = total.shape[1] // groups // HEAD
        for n in range(groups):
            for j in range(each):
                at = (n * each + j) * HEAD
                high, low = words(total[:, at : at + HEAD])
                out_ref[n, j * SLOT : (j + 1) * SLOT, :] = high
                out_ref[n, (each + j) * SLOT : (each + j + 1) * SLOT, :] = low


def feed(x, gain, gate, up, down, groups, extra):
    width, hidden = gate.shape
    tile = HEAD
    return pl.pallas_call(
        feed_kernel,
        grid=(hidden // tile,),
        in_specs=[
            pl.BlockSpec(x.shape, lambda i: (0, 0)),
            pl.BlockSpec((1, width), lambda i: (0, 0)),
            pl.BlockSpec((width, tile), lambda i: (0, i)),
            pl.BlockSpec((width, tile), lambda i: (0, i)),
            pl.BlockSpec((tile, width), lambda i: (i, 0)),
        ],
        out_specs=pl.BlockSpec((groups, extra, HEAD), lambda i: (0, 0, 0)),
        out_shape=jax.ShapeDtypeStruct((groups, extra, HEAD), jnp.bfloat16),
        scratch_shapes=[
            pltpu.VMEM((SLOT, width), jnp.bfloat16),
            pltpu.VMEM((SLOT, width), jnp.float32),
        ],
        compiler_params=vmem(56),
        cost_estimate=pl.CostEstimate(
            flops=6 * SLOT * width * hidden,
            bytes_accessed=6 * width * hidden,
            transcendentals=SLOT * hidden,
        ),
        name="feed",
    )(x, gain[None, :], gate, up, down)


def fold_kernel(parts_ref, _, out_ref):
    groups, depth, _ = parts_ref.shape
    half = depth // 2
    total = jnp.zeros((half, HEAD), jnp.float32)
    for n in range(groups):
        total = total + parts_ref[n, :half, :].astype(jnp.float32)
        total = total + parts_ref[n, half:, :].astype(jnp.float32)
    high, low = words(total)
    for n in range(groups):
        out_ref[n, :half, :] = high
        out_ref[n, half:, :] = low


def fold(parts, into):
    block = pl.BlockSpec(parts.shape, lambda i: (0, 0, 0))
    return pl.pallas_call(
        fold_kernel,
        grid=(1,),
        in_specs=[block, pl.BlockSpec(memory_space=pl.ANY)],
        out_specs=block,
        out_shape=jax.ShapeDtypeStruct(into.shape, into.dtype),
        input_output_aliases={1: 0},
        compiler_params=vmem(56),
        cost_estimate=pl.CostEstimate(
            flops=2**18, bytes_accessed=2**20, transcendentals=0
        ),
        name="fold",
    )(parts, into)


def project_kernel(x_ref, parts_ref, gain_ref, key_ref, value_ref, key_gain_ref, out_ref, text):
    h = pl.program_id(0)

    @pl.when(h == 0)
    def _():
        groups, depth, _ = parts_ref.shape
        each = depth // SLOT // 2
        count = x_ref.shape[0]
        columns = []
        for n in range(groups):
            for j in range(each):
                high = parts_ref[n, j * SLOT : (j + 1) * SLOT, :].astype(jnp.float32)
                low = parts_ref[n, (each + j) * SLOT : (each + j + 1) * SLOT, :]
                columns.append((high + low.astype(jnp.float32))[:count])
        x = x_ref[...].astype(jnp.float32) + jnp.concatenate(columns, axis=1)
        inverse = lax.rsqrt(jnp.mean(x * x, axis=-1, keepdims=True) + EPS)
        rows = x * inverse * gain_ref[...]
        spare = jnp.zeros((SLOT - count, x.shape[1]), jnp.float32)
        text[...] = jnp.concatenate([rows, spare], axis=0).astype(jnp.bfloat16)

    rows = text[...]
    keys = jnp.dot(rows, key_ref[...], preferred_element_type=jnp.float32)
    inverse = lax.rsqrt(jnp.mean(keys * keys, axis=-1, keepdims=True) + EPS)
    keys = (keys * inverse * key_gain_ref[...]).astype(jnp.bfloat16)
    values = jnp.dot(rows, value_ref[...], preferred_element_type=jnp.float32)
    values = values.astype(jnp.bfloat16)
    for n in range(out_ref.shape[0]):
        out_ref[n, :SLOT, :] = keys
        out_ref[n, SLOT:, :] = values


def project(x, parts, gain, key, value, key_gain, extra, copies):
    width, part = key.shape
    heads = part // HEAD
    weight = pl.BlockSpec((width, HEAD), lambda h: (0, h))
    return pl.pallas_call(
        project_kernel,
        grid=(heads,),
        in_specs=[
            pl.BlockSpec(x.shape, lambda h: (0, 0)),
            pl.BlockSpec((parts.shape[0], extra, HEAD), lambda h: (0, 0, 0)),
            pl.BlockSpec((1, width), lambda h: (0, 0)),
            weight,
            weight,
            pl.BlockSpec((1, HEAD), lambda h: (0, h)),
        ],
        out_specs=pl.BlockSpec((copies, 2 * SLOT, HEAD), lambda h: (0, h, 0)),
        out_shape=jax.ShapeDtypeStruct((copies, heads * 2 * SLOT, HEAD), jnp.bfloat16),
        scratch_shapes=[pltpu.VMEM((SLOT, width), jnp.bfloat16)],
        compiler_params=vmem(56),
        cost_estimate=pl.CostEstimate(
            flops=4 * SLOT * width * part, bytes_accessed=4 * width * part, transcendentals=0
        ),
        name="project",
    )(x, parts, gain[None, :], key, value, key_gain[None, :])


def attend_kernel(views, nq, nkv, ring, *refs):
    inputs, outs = refs[: len(views)], refs[len(views) : -5]
    q_s, k_s, v_s, o_s, sems = refs[-5:]
    blocks = q_s.shape[0] // nq
    copies = []
    counts = [0, 0]
    for ref, (kind, start) in zip(inputs, views):
        pieces = [ref] if len(ref.shape) == 3 else [ref.at[i] for i in range(ref.shape[0])]
        for piece in pieces:
            rows = pl.ds(counts[kind] * blocks, blocks)
            counts[kind] += 1
            targets = ((0, q_s),) if kind == 0 else ((0, k_s), (HEAD, v_s))
            for offset, scratch in targets:
                copies.append((piece.at[:, pl.ds(start + offset, HEAD), :], scratch.at[rows]))
    copies = [
        pltpu.make_async_copy(src, dst, sems.at[i]) for i, (src, dst) in enumerate(copies)
    ]
    q_copies, kv_copies = copies[:nq], copies[nq:]
    for copy in q_copies[:1] + kv_copies + q_copies[1:]:
        copy.start()
    q_copies[0].wait()
    per_q = TILE // HEAD
    per_k = CHUNK // HEAD
    per_block = blocks // per_q
    chunk_copies = 2 * per_k // blocks

    def tile(t, first):
        q = q_s[pl.ds(t * per_q, per_q)].reshape(TILE, HEAD)
        acc = jnp.zeros((HEAD, TILE), jnp.float32)
        total = jnp.zeros((8, TILE), jnp.float32)
        for j in range(nkv * blocks // per_k):
            if first is True:
                for copy in kv_copies[j * chunk_copies : (j + 1) * chunk_copies]:
                    copy.wait()
            keys = k_s[j * per_k : (j + 1) * per_k].reshape(CHUNK, HEAD)
            s = lax.dot_general(
                keys, q, (((1,), (1,)), ((), ())), preferred_element_type=jnp.float32
            )
            p = jnp.exp2(s)
            total = total + jnp.sum(p.reshape(CHUNK // 8, 8, TILE), axis=0)
            values = jnp.concatenate(
                [v_s[j * per_k + i] for i in range(per_k)], axis=1
            )
            acc = acc + jnp.dot(
                values, p.astype(jnp.bfloat16), preferred_element_type=jnp.float32
            )
        row = jnp.sum(total, axis=0, keepdims=True)
        high = row.astype(jnp.bfloat16).astype(jnp.float32)
        words = jnp.concatenate(
            [jnp.broadcast_to(high, (8, TILE)), jnp.broadcast_to(row - high, (8, TILE))], axis=0
        )
        columns = pl.ds(pl.multiple_of((t % per_block) * TILE, TILE), TILE)
        slot = t // per_block
        if ring is not None:
            slot = ring(slot)
        o_s[slot, :HEAD, columns] = acc.astype(jnp.bfloat16)
        o_s[slot, HEAD:, columns] = words.astype(jnp.bfloat16)
        return 0

    tile(0, True)
    for copy in q_copies[1:]:
        copy.wait()
    lax.fori_loop(1, nq * per_block, tile, 0)
    if ring is not None:
        copies = [pltpu.make_async_copy(o_s, outs[0], sems.at[0])]
    else:
        copies = [
            pltpu.make_async_copy(o_s.at[i], ref, sems.at[i]) for i, ref in enumerate(outs)
        ]
    for copy in copies:
        copy.start()
    for copy in copies:
        copy.wait()


def attend(queries, pairs, ring=None):
    arrays = [array for array, _ in queries + pairs]
    views = [(0, start) for _, start in queries] + [(1, start) for _, start in pairs]
    nq, nkv = (sum(math.prod(a.shape[:-3]) for a, _ in part) for part in (queries, pairs))
    blocks = arrays[0].shape[-3]
    count = blocks * HEAD
    work = nq * nkv * count * count
    shapes = [jax.ShapeDtypeStruct((HEAD + EXTRA, count), jnp.bfloat16)] * nq
    if ring is not None:
        shapes = [jax.ShapeDtypeStruct((nq, HEAD + EXTRA, count), jnp.bfloat16)]
    return pl.pallas_call(
        lambda *refs: attend_kernel(views, nq, nkv, ring, *refs),
        in_specs=[pl.BlockSpec(memory_space=pl.ANY)] * len(arrays),
        out_specs=[pl.BlockSpec(memory_space=pl.ANY)] * len(shapes),
        out_shape=shapes,
        scratch_shapes=[
            pltpu.VMEM((nq * blocks, HEAD, HEAD), jnp.bfloat16),
            pltpu.VMEM((nkv * blocks, HEAD, HEAD), jnp.bfloat16),
            pltpu.VMEM((nkv * blocks, HEAD, HEAD), jnp.bfloat16),
            pltpu.VMEM((nq, HEAD + EXTRA, count), jnp.bfloat16),
            pltpu.SemaphoreType.DMA((nq + 2 * nkv,)),
        ],
        compiler_params=vmem(56),
        cost_estimate=pl.CostEstimate(
            flops=4 * HEAD * work, bytes_accessed=6 * 2**20, transcendentals=work
        ),
        name="attend",
    )(*arrays)


def merge_kernel(sizes, *refs):
    out_ref = refs[-1]
    refs = list(refs[: sum(sizes)])
    for h, size in enumerate(sizes):
        group, refs = refs[:size], refs[size:]
        if size == 1:
            group = [group[0].at[i] for i in range(group[0].shape[0])]
        weighted = sum(ref[:HEAD, :].astype(jnp.float32) for ref in group)
        pieces = sum(ref[HEAD:, :].astype(jnp.float32) for ref in group)
        total = pieces[0:1] + pieces[8:9]
        out_ref[:, h * HEAD : (h + 1) * HEAD] = (weighted / total).T.astype(jnp.bfloat16)


def merge(results, width, column, into=None):
    heads = len(results)
    arrays = [array for group in results for array in group]
    sizes = [len(group) for group in results]
    count = arrays[0].shape[-1]
    step = 512
    specs = []
    for array in arrays:
        if array.ndim == 2:
            specs.append(pl.BlockSpec((array.shape[0], step), lambda i: (0, i)))
        else:
            specs.append(pl.BlockSpec(array.shape[:2] + (step,), lambda i: (0, 0, i)))
    aliases = {}
    if into is not None:
        aliases = {len(arrays): 0}
        arrays.append(into)
        specs.append(pl.BlockSpec(memory_space=pl.ANY))
    return pl.pallas_call(
        lambda *refs: merge_kernel(sizes, *refs),
        grid=(count // step,),
        in_specs=specs,
        out_specs=pl.BlockSpec((step, heads * HEAD), lambda i: (i, column)),
        out_shape=jax.ShapeDtypeStruct((count, width), jnp.bfloat16),
        input_output_aliases=aliases,
        compiler_params=vmem(56),
        cost_estimate=pl.CostEstimate(
            flops=count * heads * HEAD * 8, bytes_accessed=heads * 2**21, transcendentals=0
        ),
        name="merge",
    )(*arrays)


def cross_kernel(start, per, length_ref, c_ref, kv_ref, out_ref):
    live = length_ref[0]
    blocks = c_ref.shape[0]
    sources = kv_ref.shape[0]
    count = sources * SLOT
    tile = blocks * HEAD
    row = lax.broadcasted_iota(jnp.int32, (count, tile), 0)
    source, slot = row // SLOT, row % SLOT
    alive = (slot < per) & (source * per + slot < live)
    for h in range(kv_ref.shape[1] // (2 * SLOT)):
        at = 2 * h * SLOT
        keys = kv_ref[:, at : at + SLOT, :].reshape(count, HEAD)
        values = kv_ref[:, at + SLOT : at + 2 * SLOT, :].reshape(count, HEAD)
        values = values.astype(jnp.float32).T.astype(jnp.bfloat16)
        first = start + h * HEAD
        q = c_ref[:, first : first + HEAD, :].reshape(tile, HEAD)
        s = lax.dot_general(
            keys, q, (((1,), (1,)), ((), ())), preferred_element_type=jnp.float32
        )
        p = jnp.where(alive, jnp.exp2(s), 0.0)
        total = jnp.sum(p, axis=0, keepdims=True)
        weighted = jnp.dot(values, p.astype(jnp.bfloat16), preferred_element_type=jnp.float32)
        out_ref[:, h * HEAD : (h + 1) * HEAD] = (weighted / total).T.astype(jnp.bfloat16)


def cross(lengths, c, start, kv, per):
    blocks, depth, _ = c.shape
    step = 4
    heads = kv.shape[1] // (2 * SLOT)
    return pl.pallas_call(
        lambda *refs: cross_kernel(start, per, *refs),
        grid=(blocks // step,),
        in_specs=[
            pl.BlockSpec(memory_space=pltpu.SMEM),
            pl.BlockSpec((step, depth, HEAD), lambda i: (i, 0, 0)),
            pl.BlockSpec(kv.shape, lambda i: (0, 0, 0)),
        ],
        out_specs=pl.BlockSpec((step * HEAD, heads * HEAD), lambda i: (i, 0)),
        out_shape=jax.ShapeDtypeStruct((blocks * HEAD, heads * HEAD), jnp.bfloat16),
        compiler_params=vmem(56),
        cost_estimate=pl.CostEstimate(
            flops=4 * HEAD * heads * blocks * HEAD * kv.shape[0] * SLOT,
            bytes_accessed=3 * 2**20,
            transcendentals=heads * blocks * HEAD * kv.shape[0] * SLOT,
        ),
        name="cross",
    )(lengths, c, kv)


def spot(hi, z, core):
    return hi * 8 + z * 2 + core


def wide_pairs(move):
    places = [(hi, z, core) for hi in range(2) for z in range(4) for core in range(2)]
    return [(spot(*place), spot(*move(*place))) for place in places]


UP = wide_pairs(lambda hi, z, core: (hi, (z + 1) % 4, core))
DOWN = wide_pairs(lambda hi, z, core: (hi, (z + 3) % 4, core))
ACROSS = wide_pairs(lambda hi, z, core: (hi, (z + 2) % 4, core))
OTHER_X = wide_pairs(lambda hi, z, core: (1 - hi, z, core))
OTHER_CORE = wide_pairs(lambda hi, z, core: (hi, z, 1 - core))
ALONG_Z = [[spot(hi, z, core) for z in range(4)] for hi in range(2) for core in range(2)]
ALONG_X = [[spot(hi, z, core) for hi in range(2) for core in range(2)] for z in range(4)]


def send(array, pairs):
    return lax.ppermute(array, "wide", pairs)


def collect(array, groups):
    return lax.all_gather(array, "wide", axis=0, axis_index_groups=groups)


def give_back(parts):
    own, below, above, across = parts
    return [own, send(below, DOWN), send(above, UP), send(across, ACROSS)]


def trade_back(parts):
    return lax.all_to_all(
        parts, "wide", split_axis=0, concat_axis=0, axis_index_groups=ALONG_Z, tiled=True
    )


def from_ring(block):
    z = lax.axis_index("wide") // 2 % 4
    shift = jnp.where(block == 1, 3, jnp.where(block == 2, 1, jnp.where(block == 3, 2, 0)))
    return (z + shift) % 4


def around(array):
    return [send(array, UP), send(array, DOWN), send(array, ACROSS)]


def after(arrays):
    return lax.optimization_barrier(arrays)


def trade(array):
    return lax.all_to_all(array, "narrow", split_axis=0, concat_axis=0, tiled=True)


def body(
    prompt_states,
    prompt_lengths,
    feed_gain,
    gate_weight,
    up_weight,
    down_weight,
    final_gain,
    key_weight,
    value_weight,
    prompt_key_gain,
    latent_queries,
    latent_keys,
    latent_values,
    cross_queries,
    query_gain,
    key_gain,
    cross_query_gain,
):
    groups = latent_queries.shape[1] // key_weight.shape[1]
    per, width = prompt_states.shape
    extra = width // groups // HEAD * SLOT * 2
    heads = key_weight.shape[1] // HEAD
    each = 3 * HEAD
    last = heads - 1
    arrays = (latent_queries, latent_keys, latent_values, cross_queries)
    gains = (query_gain, key_gain, cross_query_gain)

    def split(traded, base, count):
        middle, end = base + 2 * count * HEAD, base + 3 * count * HEAD
        return traded[:, middle:end], traded[:, base:middle]

    early = {
        "heads": [(0, 0, 0, 4 * HEAD), (1, 0, 2 * HEAD, 5 * HEAD)],
        "crossed": [],
    }
    late = {
        "heads": [(2, 0, extra, extra + 2 * HEAD)],
        "crossed": [(h, 0, extra + (3 + h) * HEAD) for h in range(heads)],
    }

    def views(queries, pairs, h=0):
        return [(a, h * HEAD) for a in queries], [(a, 2 * h * HEAD) for a in pairs]

    (packed,) = pack(arrays, gains, groups, heads, early, [2 * each])
    traded = trade(packed)
    (final,) = pack(arrays, gains, groups, heads, late, [extra + 2 * each])
    pieces = feed(prompt_states, feed_gain, gate_weight, up_weight, down_weight, groups, extra)
    traded, pieces, final = after((traded, pieces, final))
    query, pair = split(traded, 0, 2)
    pair_x = send(pair, OTHER_X)
    queries = [query] + around(query)
    pairs = [pair, send(pair, OTHER_CORE)]
    final = fold(trade(pieces), final)
    pair_x, queries, token = after((pair_x, queries, final[:1, :16]))
    final = trade(final)
    pairs += [pair_x, send(pair_x, OTHER_CORE)]
    part0 = attend(*views(queries, pairs), from_ring)
    final, part0 = after((final, part0))
    query2, pair2 = split(final, extra, 1)
    pair_x2 = send(pair2, OTHER_X)
    queries2 = [query2] + around(query2)
    pairs2 = [pair2, send(pair2, OTHER_CORE)]
    result0 = trade_back(part0[0])
    part1 = attend(*views(queries, pairs, 1))

    tied = (part1, queries2, pair_x2, pairs2, result0, final)
    part1, queries2, pair_x2, pairs2, result0, folded = after(tied)
    pairs2 += [pair_x2, send(pair_x2, OTHER_CORE)]
    result1 = give_back(part1)
    prompt_pair = project(
        prompt_states,
        folded,
        final_gain,
        key_weight,
        value_weight,
        prompt_key_gain,
        extra,
        lax.axis_size("wide"),
    )
    prompt_pair = lax.all_to_all(prompt_pair, "wide", split_axis=0, concat_axis=0, tiled=True)
    others = attend(*views(queries2[1:], pairs2))
    result1[:3], others, prompt_pair = after((result1[:3], others, prompt_pair))
    below, above, across = others
    result2 = [send(below, DOWN), send(above, UP), send(across, ACROSS)]
    result2 += attend(*views(queries2[:1], pairs2))
    cross_out = cross(prompt_lengths, final, extra + each, prompt_pair, per)
    self_out = merge([[result0], result1], heads * HEAD, 0)
    result2, cross_out, self_out = after((result2, cross_out, self_out))
    self_out = merge([result2], heads * HEAD, last, self_out)
    return (self_out, cross_out)


def solution(mesh):
    rows = P(("wide", "narrow"), None)
    return jax.shard_map(
        body,
        mesh=mesh,
        in_specs=(
            P("wide", None),
            P(),
            P(),
            P(None, "narrow"),
            P(None, "narrow"),
            P("narrow", None),
            P(),
            P(None, "narrow"),
            P(None, "narrow"),
            P("narrow"),
            rows,
            rows,
            rows,
            rows,
            P(),
            P(),
            P(),
        ),
        out_specs=(P("wide", "narrow"), P("wide", "narrow")),
        check_vma=False,
    )
```

```python
import math

import jax
import jax.numpy as jnp
from jax import lax
from jax.experimental import pallas as pl
from jax.experimental.pallas import tpu as pltpu
from jax.sharding import PartitionSpec as P

HEAD = 128
EPS = 1e-06
SCALE = math.log2(math.e) / math.sqrt(HEAD)
TILE = 512
CHUNK = 2048
EXTRA = 16
SLOT = 32


def vmem(mib):
    return pltpu.CompilerParams(vmem_limit_bytes=mib * 2**20)


def normed(ref, gain_ref, at, factor):
    x = ref[:, at].astype(jnp.float32)
    inverse = lax.rsqrt(jnp.mean(x * x, axis=-1, keepdims=True) + EPS)
    return (x * inverse * (gain_ref[:, at] * factor)).astype(jnp.bfloat16)


def pack_kernel(heads, plan, q_ref, k_ref, v_ref, qg_ref, kg_ref, *rest):
    groups = rest[-1].shape[0]
    outs = rest[2:] if plan["crossed"] else rest

    def group(n, _):
        for h, out, pair, query in plan["heads"]:
            at = pl.ds(pl.multiple_of((n * heads + h) * HEAD, HEAD), HEAD)
            ref = outs[out]
            ref[n, pair : pair + HEAD, :] = normed(k_ref, kg_ref, at, 1.0)
            ref[n, pair + HEAD : pair + 2 * HEAD, :] = (
                v_ref[:, at].astype(jnp.float32).T.astype(jnp.bfloat16)
            )
            ref[n, query : query + HEAD, :] = normed(q_ref, qg_ref, at, SCALE)
        for h, out, base in plan["crossed"]:
            at = pl.ds(pl.multiple_of((n * heads + h) * HEAD, HEAD), HEAD)
            outs[out][n, base : base + HEAD, :] = normed(rest[0], rest[1], at, SCALE)
        return 0

    lax.fori_loop(0, groups, group, 0)


def pack(arrays, gains, groups, heads, plan, depths):
    whole = pl.BlockSpec(memory_space=pltpu.VMEM)
    operands = list(arrays[:3]) + [gain[None, :] for gain in gains[:2]]
    if plan["crossed"]:
        operands += [arrays[3], gains[2][None, :]]
    units = 3 * len(plan["heads"]) + len(plan["crossed"])
    return pl.pallas_call(
        lambda *refs: pack_kernel(heads, plan, *refs),
        in_specs=[whole] * len(operands),
        out_specs=[whole] * len(depths),
        out_shape=[
            jax.ShapeDtypeStruct((groups, depth, HEAD), jnp.bfloat16) for depth in depths
        ],
        compiler_params=vmem(56),
        cost_estimate=pl.CostEstimate(
            flops=8 * arrays[0].size, bytes_accessed=units * 2**20, transcendentals=0
        ),
        name="pack",
    )(*operands)


def words(block):
    high = block.astype(jnp.bfloat16)
    return high, (block - high.astype(jnp.float32)).astype(jnp.bfloat16)


def feed_kernel(x_ref, gain_ref, gate_ref, up_ref, down_ref, out_ref, rows_ref, total):
    step = pl.program_id(0)

    @pl.when(step == 0)
    def _():
        x = x_ref[...].astype(jnp.float32)
        inverse = lax.rsqrt(jnp.mean(x * x, axis=-1, keepdims=True) + EPS)
        rows = x * inverse * gain_ref[...]
        spare = jnp.zeros((SLOT - x.shape[0], x.shape[1]), jnp.float32)
        rows_ref[...] = jnp.concatenate([rows, spare], axis=0).astype(jnp.bfloat16)
        total[...] = jnp.zeros_like(total)

    rows = rows_ref[...]
    gate = jnp.dot(rows, gate_ref[...], preferred_element_type=jnp.float32)
    upward = jnp.dot(rows, up_ref[...], preferred_element_type=jnp.float32)
    hidden = (jax.nn.gelu(gate, approximate=True) * upward).astype(jnp.bfloat16)
    total[...] += jnp.dot(hidden, down_ref[...], preferred_element_type=jnp.float32)

    @pl.when(step == pl.num_programs(0) - 1)
    def _():
        groups = out_ref.shape[0]
        each = total.shape[1] // groups // HEAD
        for n in range(groups):
            for j in range(each):
                at = (n * each + j) * HEAD
                high, low = words(total[:, at : at + HEAD])
                out_ref[n, j * SLOT : (j + 1) * SLOT, :] = high
                out_ref[n, (each + j) * SLOT : (each + j + 1) * SLOT, :] = low


def feed(x, gain, gate, up, down, groups, extra):
    width, hidden = gate.shape
    tile = HEAD
    return pl.pallas_call(
        feed_kernel,
        grid=(hidden // tile,),
        in_specs=[
            pl.BlockSpec(x.shape, lambda i: (0, 0)),
            pl.BlockSpec((1, width), lambda i: (0, 0)),
            pl.BlockSpec((width, tile), lambda i: (0, i)),
            pl.BlockSpec((width, tile), lambda i: (0, i)),
            pl.BlockSpec((tile, width), lambda i: (i, 0)),
        ],
        out_specs=pl.BlockSpec((groups, extra, HEAD), lambda i: (0, 0, 0)),
        out_shape=jax.ShapeDtypeStruct((groups, extra, HEAD), jnp.bfloat16),
        scratch_shapes=[
            pltpu.VMEM((SLOT, width), jnp.bfloat16),
            pltpu.VMEM((SLOT, width), jnp.float32),
        ],
        compiler_params=vmem(56),
        cost_estimate=pl.CostEstimate(
            flops=6 * SLOT * width * hidden,
            bytes_accessed=6 * width * hidden,
            transcendentals=SLOT * hidden,
        ),
        name="feed",
    )(x, gain[None, :], gate, up, down)


def fold_kernel(parts_ref, _, out_ref):
    groups, depth, _ = parts_ref.shape
    half = depth // 2
    total = jnp.zeros((half, HEAD), jnp.float32)
    for n in range(groups):
        total = total + parts_ref[n, :half, :].astype(jnp.float32)
        total = total + parts_ref[n, half:, :].astype(jnp.float32)
    high, low = words(total)
    for n in range(groups):
        out_ref[n, :half, :] = high
        out_ref[n, half:, :] = low


def fold(parts, into):
    block = pl.BlockSpec(parts.shape, lambda i: (0, 0, 0))
    return pl.pallas_call(
        fold_kernel,
        grid=(1,),
        in_specs=[block, pl.BlockSpec(memory_space=pl.ANY)],
        out_specs=block,
        out_shape=jax.ShapeDtypeStruct(into.shape, into.dtype),
        input_output_aliases={1: 0},
        compiler_params=vmem(56),
        cost_estimate=pl.CostEstimate(
            flops=2**18, bytes_accessed=2**20, transcendentals=0
        ),
        name="fold",
    )(parts, into)


def project_kernel(x_ref, parts_ref, gain_ref, key_ref, value_ref, key_gain_ref, out_ref, text):
    h = pl.program_id(0)

    @pl.when(h == 0)
    def _():
        groups, depth, _ = parts_ref.shape
        each = depth // SLOT // 2
        count = x_ref.shape[0]
        columns = []
        for n in range(groups):
            for j in range(each):
                high = parts_ref[n, j * SLOT : (j + 1) * SLOT, :].astype(jnp.float32)
                low = parts_ref[n, (each + j) * SLOT : (each + j + 1) * SLOT, :]
                columns.append((high + low.astype(jnp.float32))[:count])
        x = x_ref[...].astype(jnp.float32) + jnp.concatenate(columns, axis=1)
        inverse = lax.rsqrt(jnp.mean(x * x, axis=-1, keepdims=True) + EPS)
        rows = x * inverse * gain_ref[...]
        spare = jnp.zeros((SLOT - count, x.shape[1]), jnp.float32)
        text[...] = jnp.concatenate([rows, spare], axis=0).astype(jnp.bfloat16)

    rows = text[...]
    keys = jnp.dot(rows, key_ref[...], preferred_element_type=jnp.float32)
    inverse = lax.rsqrt(jnp.mean(keys * keys, axis=-1, keepdims=True) + EPS)
    keys = (keys * inverse * key_gain_ref[...]).astype(jnp.bfloat16)
    values = jnp.dot(rows, value_ref[...], preferred_element_type=jnp.float32)
    values = values.astype(jnp.bfloat16)
    for n in range(out_ref.shape[0]):
        out_ref[n, :SLOT, :] = keys
        out_ref[n, SLOT:, :] = values


def project(x, parts, gain, key, value, key_gain, extra, copies):
    width, part = key.shape
    heads = part // HEAD
    weight = pl.BlockSpec((width, HEAD), lambda h: (0, h))
    return pl.pallas_call(
        project_kernel,
        grid=(heads,),
        in_specs=[
            pl.BlockSpec(x.shape, lambda h: (0, 0)),
            pl.BlockSpec((parts.shape[0], extra, HEAD), lambda h: (0, 0, 0)),
            pl.BlockSpec((1, width), lambda h: (0, 0)),
            weight,
            weight,
            pl.BlockSpec((1, HEAD), lambda h: (0, h)),
        ],
        out_specs=pl.BlockSpec((copies, 2 * SLOT, HEAD), lambda h: (0, h, 0)),
        out_shape=jax.ShapeDtypeStruct((copies, heads * 2 * SLOT, HEAD), jnp.bfloat16),
        scratch_shapes=[pltpu.VMEM((SLOT, width), jnp.bfloat16)],
        compiler_params=vmem(56),
        cost_estimate=pl.CostEstimate(
            flops=4 * SLOT * width * part, bytes_accessed=4 * width * part, transcendentals=0
        ),
        name="project",
    )(x, parts, gain[None, :], key, value, key_gain[None, :])


def attend_kernel(views, nq, nkv, ring, *refs):
    inputs, outs = refs[: len(views)], refs[len(views) : -5]
    q_s, k_s, v_s, o_s, sems = refs[-5:]
    blocks = q_s.shape[0] // nq
    copies = []
    counts = [0, 0]
    for ref, (kind, start) in zip(inputs, views):
        pieces = [ref] if len(ref.shape) == 3 else [ref.at[i] for i in range(ref.shape[0])]
        for piece in pieces:
            rows = pl.ds(counts[kind] * blocks, blocks)
            counts[kind] += 1
            targets = ((0, q_s),) if kind == 0 else ((0, k_s), (HEAD, v_s))
            for offset, scratch in targets:
                copies.append((piece.at[:, pl.ds(start + offset, HEAD), :], scratch.at[rows]))
    copies = [
        pltpu.make_async_copy(src, dst, sems.at[i]) for i, (src, dst) in enumerate(copies)
    ]
    q_copies, kv_copies = copies[:nq], copies[nq:]
    for copy in q_copies[:1] + kv_copies + q_copies[1:]:
        copy.start()
    q_copies[0].wait()
    per_q = TILE // HEAD
    per_k = CHUNK // HEAD
    per_block = blocks // per_q
    chunk_copies = 2 * per_k // blocks

    def tile(t, first):
        q = q_s[pl.ds(t * per_q, per_q)].reshape(TILE, HEAD)
        acc = jnp.zeros((HEAD, TILE), jnp.float32)
        total = jnp.zeros((8, TILE), jnp.float32)
        for j in range(nkv * blocks // per_k):
            if first is True:
                for copy in kv_copies[j * chunk_copies : (j + 1) * chunk_copies]:
                    copy.wait()
            keys = k_s[j * per_k : (j + 1) * per_k].reshape(CHUNK, HEAD)
            s = lax.dot_general(
                keys, q, (((1,), (1,)), ((), ())), preferred_element_type=jnp.float32
            )
            p = jnp.exp2(s)
            total = total + jnp.sum(p.reshape(CHUNK // 8, 8, TILE), axis=0)
            values = jnp.concatenate(
                [v_s[j * per_k + i] for i in range(per_k)], axis=1
            )
            acc = acc + jnp.dot(
                values, p.astype(jnp.bfloat16), preferred_element_type=jnp.float32
            )
        row = jnp.sum(total, axis=0, keepdims=True)
        high = row.astype(jnp.bfloat16).astype(jnp.float32)
        words = jnp.concatenate(
            [jnp.broadcast_to(high, (8, TILE)), jnp.broadcast_to(row - high, (8, TILE))], axis=0
        )
        columns = pl.ds(pl.multiple_of((t % per_block) * TILE, TILE), TILE)
        slot = t // per_block
        if ring is not None:
            slot = ring(slot)
        o_s[slot, :HEAD, columns] = acc.astype(jnp.bfloat16)
        o_s[slot, HEAD:, columns] = words.astype(jnp.bfloat16)
        return 0

    tile(0, True)
    for copy in q_copies[1:]:
        copy.wait()
    lax.fori_loop(1, nq * per_block, tile, 0)
    if ring is not None:
        copies = [pltpu.make_async_copy(o_s, outs[0], sems.at[0])]
    else:
        copies = [
            pltpu.make_async_copy(o_s.at[i], ref, sems.at[i]) for i, ref in enumerate(outs)
        ]
    for copy in copies:
        copy.start()
    for copy in copies:
        copy.wait()


def attend(queries, pairs, ring=None):
    arrays = [array for array, _ in queries + pairs]
    views = [(0, start) for _, start in queries] + [(1, start) for _, start in pairs]
    nq, nkv = (sum(math.prod(a.shape[:-3]) for a, _ in part) for part in (queries, pairs))
    blocks = arrays[0].shape[-3]
    count = blocks * HEAD
    work = nq * nkv * count * count
    shapes = [jax.ShapeDtypeStruct((HEAD + EXTRA, count), jnp.bfloat16)] * nq
    if ring is not None:
        shapes = [jax.ShapeDtypeStruct((nq, HEAD + EXTRA, count), jnp.bfloat16)]
    return pl.pallas_call(
        lambda *refs: attend_kernel(views, nq, nkv, ring, *refs),
        in_specs=[pl.BlockSpec(memory_space=pl.ANY)] * len(arrays),
        out_specs=[pl.BlockSpec(memory_space=pl.ANY)] * len(shapes),
        out_shape=shapes,
        scratch_shapes=[
            pltpu.VMEM((nq * blocks, HEAD, HEAD), jnp.bfloat16),
            pltpu.VMEM((nkv * blocks, HEAD, HEAD), jnp.bfloat16),
            pltpu.VMEM((nkv * blocks, HEAD, HEAD), jnp.bfloat16),
            pltpu.VMEM((nq, HEAD + EXTRA, count), jnp.bfloat16),
            pltpu.SemaphoreType.DMA((nq + 2 * nkv,)),
        ],
        compiler_params=vmem(56),
        cost_estimate=pl.CostEstimate(
            flops=4 * HEAD * work, bytes_accessed=6 * 2**20, transcendentals=work
        ),
        name="attend",
    )(*arrays)


def merge_kernel(sizes, *refs):
    out_ref = refs[-1]
    refs = list(refs[: sum(sizes)])
    for h, size in enumerate(sizes):
        group, refs = refs[:size], refs[size:]
        if size == 1:
            group = [group[0].at[i] for i in range(group[0].shape[0])]
        weighted = sum(ref[:HEAD, :].astype(jnp.float32) for ref in group)
        pieces = sum(ref[HEAD:, :].astype(jnp.float32) for ref in group)
        total = pieces[0:1] + pieces[8:9]
        out_ref[:, h * HEAD : (h + 1) * HEAD] = (weighted / total).T.astype(jnp.bfloat16)


def merge(results, width, column, into=None):
    heads = len(results)
    arrays = [array for group in results for array in group]
    sizes = [len(group) for group in results]
    count = arrays[0].shape[-1]
    step = 1024
    specs = []
    for array in arrays:
        if array.ndim == 2:
            specs.append(pl.BlockSpec((array.shape[0], step), lambda i: (0, i)))
        else:
            specs.append(pl.BlockSpec(array.shape[:2] + (step,), lambda i: (0, 0, i)))
    aliases = {}
    if into is not None:
        aliases = {len(arrays): 0}
        arrays.append(into)
        specs.append(pl.BlockSpec(memory_space=pl.ANY))
    return pl.pallas_call(
        lambda *refs: merge_kernel(sizes, *refs),
        grid=(count // step,),
        in_specs=specs,
        out_specs=pl.BlockSpec((step, heads * HEAD), lambda i: (i, column)),
        out_shape=jax.ShapeDtypeStruct((count, width), jnp.bfloat16),
        input_output_aliases=aliases,
        compiler_params=vmem(56),
        cost_estimate=pl.CostEstimate(
            flops=count * heads * HEAD * 8, bytes_accessed=heads * 2**21, transcendentals=0
        ),
        name="merge",
    )(*arrays)


def cross_kernel(per, length_ref, *refs):
    c_refs, (kv_ref, out_ref) = refs[:-2], refs[-2:]
    live = length_ref[0]
    blocks = c_refs[0].shape[0]
    sources = kv_ref.shape[0]
    count = sources * SLOT
    tile = blocks * HEAD
    row = lax.broadcasted_iota(jnp.int32, (count, tile), 0)
    source, slot = row // SLOT, row % SLOT
    alive = (slot < per) & (source * per + slot < live)
    for h, c_ref in enumerate(c_refs):
        at = 2 * h * SLOT
        keys = kv_ref[:, at : at + SLOT, :].reshape(count, HEAD)
        values = kv_ref[:, at + SLOT : at + 2 * SLOT, :].reshape(count, HEAD)
        values = values.astype(jnp.float32).T.astype(jnp.bfloat16)
        q = c_ref[...].reshape(tile, HEAD)
        s = lax.dot_general(
            keys, q, (((1,), (1,)), ((), ())), preferred_element_type=jnp.float32
        )
        p = jnp.where(alive, jnp.exp2(s), 0.0)
        total = jnp.sum(p, axis=0, keepdims=True)
        weighted = jnp.dot(values, p.astype(jnp.bfloat16), preferred_element_type=jnp.float32)
        out_ref[:, h * HEAD : (h + 1) * HEAD] = (weighted / total).T.astype(jnp.bfloat16)


def cross(lengths, c, start, kv, per):
    blocks, depth, _ = c.shape
    step = 4
    heads = kv.shape[1] // (2 * SLOT)

    def part(row):
        return pl.BlockSpec((step, HEAD, HEAD), lambda i: (i, row, 0))

    return pl.pallas_call(
        lambda *refs: cross_kernel(per, *refs),
        grid=(blocks // step,),
        in_specs=[
            pl.BlockSpec(memory_space=pltpu.SMEM),
            *[part(start // HEAD + h) for h in range(heads)],
            pl.BlockSpec(kv.shape, lambda i: (0, 0, 0)),
        ],
        out_specs=pl.BlockSpec((step * HEAD, heads * HEAD), lambda i: (i, 0)),
        out_shape=jax.ShapeDtypeStruct((blocks * HEAD, heads * HEAD), jnp.bfloat16),
        compiler_params=vmem(56),
        cost_estimate=pl.CostEstimate(
            flops=4 * HEAD * heads * blocks * HEAD * kv.shape[0] * SLOT,
            bytes_accessed=3 * 2**20,
            transcendentals=heads * blocks * HEAD * kv.shape[0] * SLOT,
        ),
        name="cross",
    )(lengths, *[c] * heads, kv)


def spot(hi, z, core):
    return hi * 8 + z * 2 + core


def wide_pairs(move):
    places = [(hi, z, core) for hi in range(2) for z in range(4) for core in range(2)]
    return [(spot(*place), spot(*move(*place))) for place in places]


UP = wide_pairs(lambda hi, z, core: (hi, (z + 1) % 4, core))
DOWN = wide_pairs(lambda hi, z, core: (hi, (z + 3) % 4, core))
ACROSS = wide_pairs(lambda hi, z, core: (hi, (z + 2) % 4, core))
OTHER_X = wide_pairs(lambda hi, z, core: (1 - hi, z, core))
OTHER_CORE = wide_pairs(lambda hi, z, core: (hi, z, 1 - core))
ALONG_Z = [[spot(hi, z, core) for z in range(4)] for hi in range(2) for core in range(2)]
ALONG_X = [[spot(hi, z, core) for hi in range(2) for core in range(2)] for z in range(4)]


def send(array, pairs):
    return lax.ppermute(array, "wide", pairs)


def collect(array, groups):
    return lax.all_gather(array, "wide", axis=0, axis_index_groups=groups)


def give_back(parts):
    own, below, above, across = parts
    return [own, send(below, DOWN), send(above, UP), send(across, ACROSS)]


def trade_back(parts):
    return lax.all_to_all(
        parts, "wide", split_axis=0, concat_axis=0, axis_index_groups=ALONG_Z, tiled=True
    )


def from_ring(block):
    z = lax.axis_index("wide") // 2 % 4
    shift = jnp.where(block == 1, 3, jnp.where(block == 2, 1, jnp.where(block == 3, 2, 0)))
    return (z + shift) % 4


def around(array):
    return [send(array, UP), send(array, DOWN), send(array, ACROSS)]


def after(arrays):
    return lax.optimization_barrier(arrays)


def trade(array):
    return lax.all_to_all(array, "narrow", split_axis=0, concat_axis=0, tiled=True)


def body(
    prompt_states,
    prompt_lengths,
    feed_gain,
    gate_weight,
    up_weight,
    down_weight,
    final_gain,
    key_weight,
    value_weight,
    prompt_key_gain,
    latent_queries,
    latent_keys,
    latent_values,
    cross_queries,
    query_gain,
    key_gain,
    cross_query_gain,
):
    groups = latent_queries.shape[1] // key_weight.shape[1]
    per, width = prompt_states.shape
    extra = width // groups // HEAD * SLOT * 2
    heads = key_weight.shape[1] // HEAD
    each = 3 * HEAD
    last = heads - 1
    arrays = (latent_queries, latent_keys, latent_values, cross_queries)
    gains = (query_gain, key_gain, cross_query_gain)

    def split(traded, base, count):
        middle, end = base + 2 * count * HEAD, base + 3 * count * HEAD
        return traded[:, middle:end], traded[:, base:middle]

    early = {
        "heads": [(0, 0, 0, 4 * HEAD), (1, 0, 2 * HEAD, 5 * HEAD)],
        "crossed": [],
    }
    late = {
        "heads": [(2, 0, extra, extra + 2 * HEAD)],
        "crossed": [(h, 0, extra + (3 + h) * HEAD) for h in range(heads)],
    }

    def views(queries, pairs, h=0):
        return [(a, h * HEAD) for a in queries], [(a, 2 * h * HEAD) for a in pairs]

    (packed,) = pack(arrays, gains, groups, heads, early, [2 * each])
    traded = trade(packed)
    (final,) = pack(arrays, gains, groups, heads, late, [extra + 2 * each])
    pieces = feed(prompt_states, feed_gain, gate_weight, up_weight, down_weight, groups, extra)
    traded, pieces, final = after((traded, pieces, final))
    query, pair = split(traded, 0, 2)
    pair_x = send(pair, OTHER_X)
    queries = [query] + around(query)
    pairs = [pair, send(pair, OTHER_CORE)]
    final = fold(trade(pieces), final)
    pair_x, queries, token = after((pair_x, queries, final[:1, :16]))
    final = trade(final)
    pairs += [pair_x, send(pair_x, OTHER_CORE)]
    part0 = attend(*views(queries, pairs), from_ring)
    final, part0 = after((final, part0))
    query2, pair2 = split(final, extra, 1)
    pair_x2 = send(pair2, OTHER_X)
    queries2 = [query2] + around(query2)
    pairs2 = [pair2, send(pair2, OTHER_CORE)]
    result0 = trade_back(part0[0])
    part1 = attend(*views(queries, pairs, 1))

    tied = (part1, queries2, pair_x2, pairs2, result0, final)
    part1, queries2, pair_x2, pairs2, result0, folded = after(tied)
    pairs2 += [pair_x2, send(pair_x2, OTHER_CORE)]
    result1 = give_back(part1)
    prompt_pair = project(
        prompt_states,
        folded,
        final_gain,
        key_weight,
        value_weight,
        prompt_key_gain,
        extra,
        lax.axis_size("wide"),
    )
    prompt_pair = lax.all_to_all(prompt_pair, "wide", split_axis=0, concat_axis=0, tiled=True)
    others = attend(*views(queries2[1:], pairs2))
    result1[:3], others, prompt_pair = after((result1[:3], others, prompt_pair))
    below, above, across = others
    result2 = [send(below, DOWN), send(above, UP), send(across, ACROSS)]
    result2 += attend(*views(queries2[:1], pairs2))
    cross_out = cross(prompt_lengths, final, extra + each, prompt_pair, per)
    self_out = merge([[result0], result1], heads * HEAD, 0)
    result2, cross_out, self_out = after((result2, cross_out, self_out))
    self_out = merge([result2], heads * HEAD, last, self_out)
    return (self_out, cross_out)


def solution(mesh):
    rows = P(("wide", "narrow"), None)
    return jax.shard_map(
        body,
        mesh=mesh,
        in_specs=(
            P("wide", None),
            P(),
            P(),
            P(None, "narrow"),
            P(None, "narrow"),
            P("narrow", None),
            P(),
            P(None, "narrow"),
            P(None, "narrow"),
            P("narrow"),
            rows,
            rows,
            rows,
            rows,
            P(),
            P(),
            P(),
        ),
        out_specs=(P("wide", "narrow"), P("wide", "narrow")),
        check_vma=False,
    )
```
